256 devices in a mesh: cfg: 2 (over x_lo), gx: 16 (over x_hi, y, core), gy: 8 (over z).
Axes of the slice: x: 4 (x_hi: 2, x_lo: 2; x = x_hi * 2 + x_lo), y: 4, z: 8, core: 2. Of those that a mesh axis runs over, the one named last changes fastest.
Arguments:
- latent: float32 [64, 128, 32, 128], P('gx', 'gy'), may hold values from -6 to 6
- sample_noise: bfloat16 [2, 64, 128, 32, 128], P(None, 'gx', 'gy'), may hold values from -6 to 6
- cond_field: bfloat16 [64, 128, 8, 128], P('gx', 'gy'), may hold values from -6 to 6
- timesteps: int32 [3], replicated, may hold values from 301 to 599, as said below
- spatial_weight: bfloat16 [3, 3, 128, 32], replicated, may hold values from -0.375 to 0.375
- cond_weight: bfloat16 [128, 8], replicated, may hold values from -2 to 2
- temporal_weight: bfloat16 [3, 32, 128], replicated, may hold values from -0.3125 to 0.3125
Outputs:
- sampled: float32 [64, 128, 32, 128], P('gx', 'gy')
The draws below stay inside these ranges and needn't reach their ends.
Inputs may be any that keep to these rules, and one draw needn't show every extreme that they name: `timesteps`: strictly falling, the first is 599, each later one 60 to 149 below the one before.
All inputs are finite; a program needn't handle non-finite values.
Results may differ from the reference program's by a relative error of at most 0.012.
Values may be sent and summed in bfloat16 or wider, within the bound.
No kernel may reach another device: no remote copies, remote signals or barrier semaphores. Data moves between devices by JAX's collectives and lax.ppermute only.
A program may use at most 128 MiB of HBM per device.

```python
import jax
import jax.numpy as jnp
from jax import lax

C = 32
FF = 128
CK = 8
NT = 128
STEPS = 2
NX = 64
NY = 128


def draw_timesteps(key, part):
    key = jax.random.fold_in(key, 11)
    first_step = jnp.full((1,), 599, jnp.int32)
    step_gaps = jax.random.randint(jax.random.fold_in(key, 12), (STEPS,), 60, 150)
    return jnp.concatenate([first_step, first_step - jnp.cumsum(step_gaps)]).astype(jnp.int32)


def shard_levels(key, extent, cuts, least, largest):
    def one(dim, parts):
        steps = jax.random.uniform(jax.random.fold_in(jax.random.fold_in(key, 6), dim), (parts,), jnp.float32, least / len(cuts), largest / len(cuts))
        return jnp.repeat(jnp.exp(steps), extent[dim] // parts).reshape((-1,) + (1,) * (len(extent) - dim - 1))

    factor_of = one(*cuts[0])
    for cut in cuts[1:]:
        factor_of = factor_of * one(*cut)
    return factor_of


def centred(rng, dims, scale, reach, pieces=(), held_as=jnp.bfloat16):
    entries = scale * jax.random.normal(rng, dims, jnp.float32)
    if pieces:
        entries = entries * shard_levels(rng, dims, pieces, -0.22, 0.18)
    return jnp.clip(entries, -reach, reach).astype(held_as)


def setup_inputs(seed: int = 0) -> dict:
    key_list = jax.random.split(jax.random.key(seed), 8)
    latent = centred(key_list[0], (NX, NY, C, NT), 1.0, 6.0, ((0, 16), (1, 8)), jnp.float32)
    sample_noise = centred(key_list[1], (STEPS, NX, NY, C, NT), 1.0, 6.0, ((1, 16), (2, 8)))
    cond_field = centred(key_list[2], (NX, NY, CK, NT), 1.0, 6.0, ((0, 16), (1, 8)))
    timesteps = draw_timesteps(jax.random.fold_in(key_list[7], 71), 0)
    spatial_weight = centred(key_list[4], (3, 3, FF, C), (9 * C) ** -0.5, 0.375)
    cond_weight = centred(key_list[5], (FF, CK), CK ** -0.5, 2.0)
    temporal_weight = centred(key_list[6], (3, C, FF), (3 * FF) ** -0.5, 0.3125)
    return dict(latent=latent, sample_noise=sample_noise, cond_field=cond_field, timesteps=timesteps, spatial_weight=spatial_weight, cond_weight=cond_weight, temporal_weight=temporal_weight)


GUIDANCE = 3.0
DDIM_ETA = 0.5

def alpha_table():
    positions = jnp.arange(1000, dtype=jnp.int32)
    beta_values = 0.0001 + (0.02 - 0.0001) * positions.astype(jnp.float32) / 999.0
    return (positions, jnp.exp(jnp.cumsum(jnp.log(1.0 - beta_values))))

def lookup(positions, table, when):
    return jnp.sum(jnp.where(positions == when, table, jnp.float32(0.0)))

def ddim_update(current, guided, fresh_noise, alpha_now, alpha_next):
    clean_estimate = (current - jnp.sqrt(1.0 - alpha_now) * guided) / jnp.sqrt(alpha_now)
    noise_scale = DDIM_ETA * jnp.sqrt((1.0 - alpha_next) / (1.0 - alpha_now)) * jnp.sqrt(1.0 - alpha_now / alpha_next)
    return jnp.sqrt(alpha_next) * clean_estimate + jnp.sqrt(1.0 - alpha_next - noise_scale * noise_scale) * guided + noise_scale * fresh_noise.astype(jnp.float32)

def finish(summed, normed, temporal_weight):
    hidden = jax.nn.silu(summed).astype(jnp.bfloat16)
    length = hidden.shape[-1]
    shifted = jnp.pad(hidden, ((0, 0), (0, 0), (1, 1)))
    output_sum = normed
    for tap_index in range(3):
        output_sum = output_sum + jnp.einsum('yft,cf->yct', shifted[:, :, tap_index:tap_index + length].astype(jnp.float32), temporal_weight[tap_index].astype(jnp.float32))
    return output_sum.astype(jnp.bfloat16)

def reference(latent, sample_noise, cond_field, timesteps, spatial_weight, cond_weight, temporal_weight):
    positions, table = alpha_table()
    current = latent
    for step_index in range(STEPS):
        alpha_now = lookup(positions, table, timesteps[step_index])
        alpha_next = lookup(positions, table, timesteps[step_index + 1])
        normed = current * lax.rsqrt(lax.optimization_barrier(jnp.mean(current * current, axis=(2, 3), keepdims=True)) + 1e-05)
        act = jax.nn.silu(normed).astype(jnp.bfloat16)
        padded = jnp.pad(act, ((1, 1), (1, 1), (0, 0), (0, 0)))

        def row_eps(row_index):
            row_block = lax.dynamic_slice_in_dim(padded, row_index, 3, 0)
            summed = jnp.zeros((NY, FF, NT), jnp.float32)
            for row_off in range(3):
                for col_off in range(3):
                    summed = summed + jnp.einsum('yct,fc->yft', row_block[row_off, col_off:col_off + NY].astype(jnp.float32), spatial_weight[row_off, col_off].astype(jnp.float32))
            cond_row = lax.dynamic_index_in_dim(cond_field, row_index, 0, keepdims=False)
            cond_term = jnp.einsum('ykt,fk->yft', cond_row.astype(jnp.float32), cond_weight.astype(jnp.float32))
            normed_row = lax.dynamic_index_in_dim(normed, row_index, 0, keepdims=False)
            return (finish(summed + cond_term, normed_row, temporal_weight), finish(summed, normed_row, temporal_weight))
        eps_cond, eps_free = lax.map(row_eps, jnp.arange(NX, dtype=jnp.int32))
        free_value = eps_free.astype(jnp.float32)
        guided = free_value + GUIDANCE * (eps_cond.astype(jnp.float32) - free_value)
        current = ddim_update(current, guided, sample_noise[step_index], alpha_now, alpha_next)
    return current
```

```python
import jax
import jax.numpy as jnp
from jax import lax
from jax.experimental import pallas as pl
from jax.experimental.pallas import tpu as pltpu
from jax.sharding import PartitionSpec as P

F32 = jnp.float32
BF16 = jnp.bfloat16
AXES = ("cfg", "gx", "gy")
NCFG, NGX, NGY = 2, 16, 8
ROWS, COLS, C, FF, CK, NT = 4, 16, 32, 128, 8, 128
YROWS = 2 * C + C + 2 * CK
XROWS = 2 * COLS * C + COLS * C + COLS * CK
DROWS = 8 * C + 2 * C + 2 * CK


def linear(cfg, gx, gy):
    return (cfg * NGX + gx) * NGY + gy


def swaps_x(parity):
    pairs = []
    for cfg in range(NCFG):
        for gy in range(NGY):
            for gx in range(parity, NGX - 1, 2):
                other = 1 - cfg if gx == NGX // 2 - 1 else cfg
                a, b = linear(cfg, gx, gy), linear(other, gx + 1, gy)
                pairs += [(a, b), (b, a)]
    return pairs


def swaps_y(parity):
    pairs = []
    for cfg in range(NCFG):
        for gx in range(NGX):
            for gy in range(parity, NGY - 1, 2):
                a, b = linear(cfg, gx, gy), linear(cfg, gx, gy + 1)
                pairs += [(a, b), (b, a)]
    return pairs


def vmem():
    return pl.BlockSpec(memory_space=pltpu.VMEM)


def smem():
    return pl.BlockSpec(memory_space=pltpu.SMEM)


def join16(*parts):
    return jnp.concatenate([p.astype(F32) for p in parts], axis=0).astype(BF16)


def pack_kernel(place, lat, noise, cond, ya, yb, xa, xb):
    def pack_y(out, high):
        lo, inner = (COLS - 2, COLS - 1) if high else (0, 0)
        for r in range(ROWS):
            out[r, 0 : 2 * C, :] = lat[r, lo : lo + 2].reshape(2 * C, NT).astype(BF16)
            out[r, 2 * C : 3 * C, :] = noise[0, r, inner]
            cell = cond[r, inner * CK : (inner + 1) * CK, :]
            out[r, 3 * C :, :] = join16(cell, cell)

    def pack_x(out, high):
        lo, inner = (ROWS - 2, ROWS - 1) if high else (0, 0)
        n = COLS * C
        for i in range(2):
            out[i * n : (i + 1) * n, :] = lat[lo + i].reshape(n, NT).astype(BF16)
        out[2 * n : 3 * n, :] = noise[0, inner].reshape(n, NT)
        out[3 * n :, :] = cond[inner]

    for parity in range(2):

        @pl.when(place[1] == parity)
        def _():
            pack_y(ya, parity == 0)
            pack_y(yb, parity == 1)

    for parity in range(2):

        @pl.when(place[0] == parity)
        def _():
            pack_x(xa, parity == 0)
            pack_x(xb, parity == 1)


def pack(place, lat, noise, cond):
    y = jax.ShapeDtypeStruct((ROWS, YROWS, NT), BF16)
    x = jax.ShapeDtypeStruct((XROWS, NT), BF16)
    return pl.pallas_call(
        pack_kernel,
        out_shape=(y, y, x, x),
        in_specs=[smem(), vmem(), vmem(), vmem()],
        out_specs=(vmem(),) * 4,
        compiler_params=pltpu.CompilerParams(vmem_limit_bytes=16 << 20),
        cost_estimate=pl.CostEstimate(flops=1 << 18, bytes_accessed=3 << 20, transcendentals=0),
        name="pack_faces",
    )(place, lat, noise, cond)


def corner_kernel(place, ya, yb, da, db):
    def pack_corner(out, low, high, top):
        lo, inner = (ROWS - 2, ROWS - 1) if top else (0, 0)
        for i in range(2):
            out[4 * C * i : 4 * C * i + 2 * C, :] = low[lo + i, 0 : 2 * C, :]
            out[4 * C * i + 2 * C : 4 * C * i + 4 * C, :] = high[lo + i, 0 : 2 * C, :]
        out[8 * C : 9 * C, :] = low[inner, 2 * C : 3 * C, :]
        out[9 * C : 10 * C, :] = high[inner, 2 * C : 3 * C, :]
        first = low[inner, 3 * C :, :].astype(F32)[0:CK]
        second = high[inner, 3 * C :, :].astype(F32)[0:CK]
        out[10 * C :, :] = join16(first, second)

    for px in range(2):
        for py in range(2):

            @pl.when((place[0] == px) & (place[1] == py))
            def _():
                low, high = (yb, ya) if py == 0 else (ya, yb)
                pack_corner(da, low, high, px == 0)
                pack_corner(db, low, high, px == 1)


def pack_corners(place, ya, yb):
    d = jax.ShapeDtypeStruct((DROWS, NT), BF16)
    return pl.pallas_call(
        corner_kernel,
        out_shape=(d, d),
        in_specs=[smem(), vmem(), vmem()],
        out_specs=(vmem(),) * 2,
        compiler_params=pltpu.CompilerParams(vmem_limit_bytes=16 << 20),
        cost_estimate=pl.CostEstimate(flops=1 << 12, bytes_accessed=1 << 18, transcendentals=0),
        name="pack_corners",
    )(place, ya, yb)


def weights_kernel(spatial, cond, temporal, wide, wide_cond, wide_temporal):
    blank = jnp.zeros((FF, C), F32)
    for dx in range(3):
        taps = [spatial[dx, dy].astype(F32) for dy in range(3)]
        wide[0:FF, dx * 4 * C : (dx + 1) * 4 * C] = jnp.concatenate(taps + [blank], axis=1).astype(BF16)
        wide[FF:, dx * 4 * C : (dx + 1) * 4 * C] = jnp.concatenate([blank] + taps, axis=1).astype(BF16)
    small = cond[...].astype(F32)
    none = jnp.zeros((FF, CK), F32)
    wide_cond[0:FF, :] = jnp.concatenate([small, none], axis=1).astype(BF16)
    wide_cond[FF:, :] = jnp.concatenate([none, small], axis=1).astype(BF16)
    wide_temporal[...] = jnp.zeros(wide_temporal.shape, BF16)
    wide_temporal[0 : 3 * C, 0:FF] = temporal[...].reshape(3 * C, FF)
    wide_temporal[3 * C :, FF:] = temporal[...].reshape(3 * C, FF)


def widen(spatial, cond, temporal):
    return pl.pallas_call(
        weights_kernel,
        out_shape=(
            jax.ShapeDtypeStruct((2 * FF, 12 * C), BF16),
            jax.ShapeDtypeStruct((2 * FF, 2 * CK), BF16),
            jax.ShapeDtypeStruct((6 * C, 2 * FF), BF16),
        ),
        in_specs=[vmem()] * 3,
        out_specs=(vmem(),) * 3,
        compiler_params=pltpu.CompilerParams(vmem_limit_bytes=16 << 20),
        cost_estimate=pl.CostEstimate(flops=1 << 18, bytes_accessed=1 << 20, transcendentals=0),
        name="widen_weights",
    )(spatial, cond, temporal)


def log_alpha(when):
    shape = (8, 128)
    position = lax.broadcasted_iota(jnp.int32, shape, 0) * 128 + lax.broadcasted_iota(jnp.int32, shape, 1)
    beta = 0.0001 + (0.02 - 0.0001) * position.astype(F32) / 999.0
    logs = jnp.log(1.0 - jnp.minimum(beta, 0.5))
    return jnp.sum(jnp.where(position <= when, logs, 0.0))


def coefficients(now, later):
    a = jnp.exp(jnp.full((1, NT), log_alpha(now), F32))
    p = jnp.exp(jnp.full((1, NT), log_alpha(later), F32))
    sigma = 0.5 * jnp.sqrt((1.0 - p) / (1.0 - a)) * jnp.sqrt(1.0 - a / p)
    keep = jnp.sqrt(p) / jnp.sqrt(a)
    move = jnp.sqrt(1.0 - p - sigma * sigma) - keep * jnp.sqrt(1.0 - a)
    return keep, move, sigma


def silu(v):
    half = 0.5 * v
    return half + half * jnp.tanh(half)


def normalize(x):
    mean = jnp.sum(jnp.sum(x * x, axis=1, keepdims=True), axis=2, keepdims=True) * (1.0 / (C * NT))
    return x * lax.rsqrt(mean + 1e-05)


def block(act, row, cond_rows, pairs, wide, wide_cond, wide_temporal):
    windows = [
        jnp.concatenate([act[row + dx, 2 * C * p : 2 * C * p + 4 * C, :] for dx in range(3)], axis=0)
        for p in pairs
    ]
    fields = [cond_rows(p) for p in pairs]
    rhs = jnp.concatenate(windows, axis=1) if len(pairs) > 1 else windows[0]
    field = jnp.concatenate(fields, axis=1) if len(pairs) > 1 else fields[0]
    free = jnp.dot(wide[...], rhs, preferred_element_type=F32)
    with_cond = free + jnp.dot(wide_cond[...], field, preferred_element_type=F32)
    hidden = (3.0 * silu(with_cond) - 2.0 * silu(free)).astype(BF16)
    taps = jnp.dot(wide_temporal[...], hidden, preferred_element_type=F32)
    time = lax.broadcasted_iota(jnp.int32, (C, NT), 1)
    sums = []
    for q in range(len(pairs)):
        for o in range(2):
            t = taps[3 * C * o : 3 * C * (o + 1), NT * q : NT * (q + 1)]
            before = jnp.where(time == 0, 0.0, pltpu.roll(t[0:C], 1, 1))
            after = jnp.where(time == NT - 1, 0.0, pltpu.roll(t[2 * C :], NT - 1, 1))
            sums.append(before + t[C : 2 * C] + after)
    return sums


def main_kernel(
    place, steps, lat, noise, cond, ya, yb, xa, xb, da, db, wide, wide_cond, wide_temporal,
    out, act, base, condx, act2,
):
    keep, move, sigma = coefficients(steps[0], steps[1])
    even_x, even_y = place[0] == 0, place[1] == 0

    def side(even, a, b, high):
        return jnp.where(even, a, b) if high else jnp.where(even, b, a)

    def prepare(e, x, fresh, field):
        normed = normalize(x)
        act[e] = silu(normed).astype(BF16).reshape(20 * C, NT)
        if fresh is not None:
            value = keep * x[1:19] + move * normed[1:19] + sigma * fresh
            base[e - 1] = value.reshape(18 * C, NT)
            condx[e - 1] = field

    def cells(v):
        return v.astype(F32).reshape(-1, C, NT)

    for r in range(ROWS):
        low = side(even_y, ya[r], yb[r], False)
        high = side(even_y, ya[r], yb[r], True)
        x = jnp.concatenate([cells(low[0 : 2 * C]), lat[r], cells(high[0 : 2 * C])], axis=0)
        fresh = jnp.concatenate(
            [cells(low[2 * C : 3 * C]), noise[0, r].astype(F32), cells(high[2 * C : 3 * C])], axis=0
        )
        field = join16(low.astype(F32)[3 * C : 3 * C + CK], cond[r], high.astype(F32)[3 * C : 3 * C + CK])
        prepare(r + 2, x, fresh, field)
    n = COLS * C
    for top in (False, True):
        face = lambda lo, hi: side(even_x, xa[lo:hi, :], xb[lo:hi, :], top)
        corner = lambda lo, hi: side(even_x, da[lo:hi, :], db[lo:hi, :], top)
        for i in range(2):
            x = jnp.concatenate(
                [
                    cells(corner(4 * C * i, 4 * C * i + 2 * C)),
                    cells(face(i * n, (i + 1) * n)),
                    cells(corner(4 * C * i + 2 * C, 4 * C * i + 4 * C)),
                ],
                axis=0,
            )
            fresh = field = None
            if i == (0 if top else 1):
                fresh = jnp.concatenate(
                    [
                        cells(corner(8 * C, 9 * C)),
                        cells(face(2 * n, 3 * n)),
                        cells(corner(9 * C, 10 * C)),
                    ],
                    axis=0,
                )
                ends = corner(10 * C, 10 * C + 2 * CK).astype(F32)
                field = join16(ends[0:CK], face(3 * n, 3 * n + COLS * CK), ends[CK:])
            prepare((6 if top else 0) + i, x, fresh, field)

    def first(e, carry):
        for lo in range(0, 9, 2):
            pairs = list(range(lo, min(lo + 2, 9)))
            sums = block(
                act, e, lambda p: condx[e, 2 * CK * p : 2 * CK * (p + 1), :], pairs, wide, wide_cond, wide_temporal
            )
            for i, s in enumerate(sums):
                at = pl.ds((2 * lo + i) * C, C)
                base[e, at, :] = base[e, at, :] + move * s
        return carry

    lax.fori_loop(0, 6, first, 0)

    keep2, move2, sigma2 = coefficients(steps[1], steps[2])
    left = jnp.where(place[3] == 0, 0.0, 1.0)
    right = jnp.where(place[3] == NGY - 1, 0.0, 1.0)
    for e in range(6):
        x = base[e].reshape(18, C, NT)
        normed = normalize(x)
        value = silu(normed)
        value = jnp.concatenate([value[0:1] * left, value[1:17], value[17:18] * right], axis=0)
        if e == 0:
            value = value * jnp.where(place[2] == 0, 0.0, 1.0)
        if e == 5:
            value = value * jnp.where(place[2] == NGX - 1, 0.0, 1.0)
        act2[e] = value.astype(BF16).reshape(18 * C, NT)
        if 0 < e < 5:
            out[e - 1] = keep2 * x[1:17] + move2 * normed[1:17] + sigma2 * noise[1, e - 1].astype(F32)

    def second(r, carry):
        for lo in range(0, 8, 2):
            sums = block(
                act2, r, lambda p: cond[r, 2 * CK * p : 2 * CK * (p + 1), :], [lo, lo + 1],
                wide, wide_cond, wide_temporal,
            )
            for i, s in enumerate(sums):
                out[r, 2 * lo + i] = out[r, 2 * lo + i] + move2 * s
        return carry

    lax.fori_loop(0, ROWS, second, 0)


def sample(place, steps, lat, noise, cond, halos, weights):
    return pl.pallas_call(
        main_kernel,
        out_shape=jax.ShapeDtypeStruct((ROWS, COLS, C, NT), F32),
        in_specs=[smem(), smem()] + [vmem()] * 12,
        out_specs=vmem(),
        scratch_shapes=[
            pltpu.VMEM((8, 20 * C, NT), BF16),
            pltpu.VMEM((6, 18 * C, NT), F32),
            pltpu.VMEM((6, 18 * CK, NT), BF16),
            pltpu.VMEM((6, 18 * C, NT), BF16),
        ],
        compiler_params=pltpu.CompilerParams(vmem_limit_bytes=40 << 20),
        cost_estimate=pl.CostEstimate(flops=2 << 30, bytes_accessed=5 << 20, transcendentals=5 << 20),
        name="sample_slab",
    )(place, steps, lat, noise, cond, *halos, *weights)


def on_device(latent, sample_noise, cond_field, timesteps, spatial_weight, cond_weight, temporal_weight):
    gx, gy = lax.axis_index("gx"), lax.axis_index("gy")
    place = jnp.stack([gx % 2, gy % 2, gx, gy]).astype(jnp.int32)
    cond = cond_field.reshape(ROWS, COLS * CK, NT)
    ya, yb, xa, xb = pack(place, latent, sample_noise, cond)
    ya = lax.ppermute(ya, AXES, swaps_y(0))
    yb = lax.ppermute(yb, AXES, swaps_y(1))
    xa = lax.ppermute(xa, AXES, swaps_x(0))
    xb = lax.ppermute(xb, AXES, swaps_x(1))
    weights = widen(spatial_weight, cond_weight, temporal_weight)
    da, db = pack_corners(place, ya, yb)
    da = lax.ppermute(da, AXES, swaps_x(0))
    db = lax.ppermute(db, AXES, swaps_x(1))
    return sample(place, timesteps, latent, sample_noise, cond, (ya, yb, xa, xb, da, db), weights)


def solution(mesh):
    in_specs = (
        P("gx", "gy", None, None),
        P(None, "gx", "gy", None, None),
        P("gx", "gy", None, None),
        P(),
        P(),
        P(),
        P(),
    )
    return jax.shard_map(
        on_device, mesh=mesh, in_specs=in_specs, out_specs=P("gx", "gy", None, None), check_vma=False
    )
```

```python
import jax
import jax.numpy as jnp
from jax import lax
from jax.experimental import pallas as pl
from jax.experimental.pallas import tpu as pltpu
from jax.sharding import PartitionSpec as P

F32 = jnp.float32
BF16 = jnp.bfloat16
VMEM_ALL = 60 << 20
AXES = ("cfg", "gx", "gy")
NCFG, NGX, NGY = 2, 16, 8
ROWS, COLS, C, FF, CK, NT = 4, 16, 32, 128, 8, 128
YROWS = 2 * C + C + 2 * CK
WIDE, MID = COLS + 4, COLS + 2
XROWS = 2 * WIDE * C + MID * C + MID * CK


def linear(cfg, gx, gy):
    return (cfg * NGX + gx) * NGY + gy


def swaps_x(parity):
    pairs = []
    for cfg in range(NCFG):
        for gy in range(NGY):
            for gx in range(parity, NGX - 1, 2):
                other = 1 - cfg if gx == NGX // 2 - 1 else cfg
                a, b = linear(cfg, gx, gy), linear(other, gx + 1, gy)
                pairs += [(a, b), (b, a)]
    return pairs


def swaps_y(parity):
    pairs = []
    for cfg in range(NCFG):
        for gx in range(NGX):
            for gy in range(parity, NGY - 1, 2):
                a, b = linear(cfg, gx, gy), linear(cfg, gx, gy + 1)
                pairs += [(a, b), (b, a)]
    return pairs


def vmem():
    return pl.BlockSpec(memory_space=pltpu.VMEM)


def smem():
    return pl.BlockSpec(memory_space=pltpu.SMEM)


def join16(*parts):
    return jnp.concatenate([p.astype(F32) for p in parts], axis=0).astype(BF16)


def any_space():
    return pl.BlockSpec(memory_space=pl.ANY)


def cells(v):
    return v.astype(F32).reshape(-1, C, NT)


def pack_y_kernel(place, lat, noise, cond, ya, yb, xs, ns, cs, sems):
    copies = []
    for side, (lo, inner, field) in enumerate(((0, 0, 0), (COLS - 2, COLS - 1, (COLS - 2) * CK))):
        copies.append(pltpu.make_async_copy(lat.at[:, lo : lo + 2], xs.at[side], sems.at[3 * side]))
        copies.append(pltpu.make_async_copy(noise.at[0, :, inner], ns.at[side], sems.at[3 * side + 1]))
        copies.append(
            pltpu.make_async_copy(cond.at[:, field : field + 2 * CK, :], cs.at[side], sems.at[3 * side + 2])
        )
    for copy in copies:
        copy.start()
    for copy in copies:
        copy.wait()

    def pack_y(out, side):
        for r in range(ROWS):
            out[r, 0 : 2 * C, :] = xs[side, r].reshape(2 * C, NT).astype(BF16)
            out[r, 2 * C : 3 * C, :] = ns[side, r]
            both = cs[side, r].astype(F32)
            cell = both[CK:] if side else both[0:CK]
            out[r, 3 * C :, :] = join16(cell, cell)

    for parity in range(2):

        @pl.when(place[1] == parity)
        def _():
            pack_y(ya, 1 - parity)
            pack_y(yb, parity)


def pack_y(place, lat, noise, cond):
    y = jax.ShapeDtypeStruct((ROWS, YROWS, NT), BF16)
    return pl.pallas_call(
        pack_y_kernel,
        out_shape=(y, y),
        in_specs=[smem(), any_space(), any_space(), any_space()],
        out_specs=(vmem(),) * 2,
        scratch_shapes=[
            pltpu.VMEM((2, ROWS, 2, C, NT), F32),
            pltpu.VMEM((2, ROWS, C, NT), BF16),
            pltpu.VMEM((2, ROWS, 2 * CK, NT), BF16),
            pltpu.SemaphoreType.DMA((6,)),
        ],
        compiler_params=pltpu.CompilerParams(vmem_limit_bytes=VMEM_ALL),
        cost_estimate=pl.CostEstimate(flops=1 << 16, bytes_accessed=1 << 19, transcendentals=0),
        name="pack_columns",
    )(place, lat, noise, cond)


def halo_columns(place, ya, yb):
    even = place[1] == 0
    return (
        lambda r: jnp.where(even, yb[r], ya[r]),
        lambda r: jnp.where(even, ya[r], yb[r]),
    )


def wide_latent(lat_row, low, high):
    return jnp.concatenate([cells(low[0 : 2 * C]), lat_row, cells(high[0 : 2 * C])], axis=0)


def wide_noise(noise_row, low, high):
    return jnp.concatenate(
        [cells(low[2 * C : 3 * C]), noise_row.astype(F32), cells(high[2 * C : 3 * C])], axis=0
    )


def wide_cond_row(cond_row, low, high):
    return join16(low.astype(F32)[3 * C : 3 * C + CK], cond_row, high.astype(F32)[3 * C : 3 * C + CK])


def pack_x_kernel(place, lat, noise, cond, ya, yb, xa, xb, token):
    lows, highs = halo_columns(place, ya, yb)

    def pack_x(out, top):
        lo, inner = (ROWS - 2, ROWS - 1) if top else (0, 0)
        n = WIDE * C
        for i in range(2):
            low, high = lows(lo + i), highs(lo + i)
            out[i * n : (i + 1) * n, :] = wide_latent(lat[lo + i], low, high).astype(BF16).reshape(n, NT)
            if lo + i == inner:
                out[2 * n : 2 * n + MID * C, :] = (
                    wide_noise(noise[0, inner], low, high).astype(BF16).reshape(MID * C, NT)
                )
                out[2 * n + MID * C :, :] = wide_cond_row(cond[inner], low, high)

    for parity in range(2):

        @pl.when(place[0] == parity)
        def _():
            pack_x(xa, parity == 0)
            pack_x(xb, parity == 1)

    token[...] = jnp.zeros(token.shape, F32)


def pack_x(place, lat, noise, cond, ya, yb):
    x = jax.ShapeDtypeStruct((XROWS, NT), BF16)
    return pl.pallas_call(
        pack_x_kernel,
        out_shape=(x, x, jax.ShapeDtypeStruct((8, NT), F32)),
        in_specs=[smem()] + [vmem()] * 5,
        out_specs=(vmem(),) * 3,
        compiler_params=pltpu.CompilerParams(vmem_limit_bytes=24 << 20),
        cost_estimate=pl.CostEstimate(flops=1 << 18, bytes_accessed=3 << 20, transcendentals=0),
        name="pack_rows",
    )(place, lat, noise, cond, ya, yb)


def weights_kernel(spatial, cond, temporal, wide, wide_cond, wide_temporal):
    blank = jnp.zeros((C, FF), F32)
    for dx in range(3):
        taps = [0.5 * spatial[dx, dy].astype(F32) for dy in range(3)]
        at = slice(dx * 4 * C, (dx + 1) * 4 * C)
        wide[0:FF, at] = jnp.concatenate(taps + [blank], axis=0).T.astype(BF16)
        wide[FF:, at] = jnp.concatenate([blank] + taps, axis=0).T.astype(BF16)
    small = 0.5 * cond[...].astype(F32)
    none = jnp.zeros((FF - CK, FF), F32)
    pair = jnp.concatenate([small, none], axis=0).T[:, 0:CK]
    gap = jnp.zeros((FF, CK), F32)
    wide_cond[0:FF, :] = jnp.concatenate([pair, gap], axis=1).astype(BF16)
    wide_cond[FF:, :] = jnp.concatenate([gap, pair], axis=1).astype(BF16)
    wide_temporal[...] = jnp.zeros(wide_temporal.shape, BF16)
    wide_temporal[0 : 3 * C, 0:FF] = (2.0 * temporal[...].astype(F32)).astype(BF16).reshape(3 * C, FF)
    wide_temporal[3 * C :, FF:] = (2.0 * temporal[...].astype(F32)).astype(BF16).reshape(3 * C, FF)


def widen(spatial, cond, temporal):
    return pl.pallas_call(
        weights_kernel,
        out_shape=(
            jax.ShapeDtypeStruct((2 * FF, 12 * C), BF16),
            jax.ShapeDtypeStruct((2 * FF, 2 * CK), BF16),
            jax.ShapeDtypeStruct((6 * C, 2 * FF), BF16),
        ),
        in_specs=[vmem()] * 3,
        out_specs=(vmem(),) * 3,
        compiler_params=pltpu.CompilerParams(vmem_limit_bytes=16 << 20),
        cost_estimate=pl.CostEstimate(flops=1 << 18, bytes_accessed=1 << 20, transcendentals=0),
        name="widen_weights",
    )(spatial, cond, temporal)


def log_alpha(when):
    shape = (8, 128)
    position = lax.broadcasted_iota(jnp.int32, shape, 0) * 128 + lax.broadcasted_iota(jnp.int32, shape, 1)
    beta = 0.0001 + (0.02 - 0.0001) * position.astype(F32) / 999.0
    logs = jnp.log(1.0 - jnp.minimum(beta, 0.5))
    return jnp.sum(jnp.where(position <= when, logs, 0.0))


def coefficients(now, later):
    a = jnp.exp(jnp.full((1, NT), log_alpha(now), F32))
    p = jnp.exp(jnp.full((1, NT), log_alpha(later), F32))
    sigma = 0.5 * jnp.sqrt((1.0 - p) / (1.0 - a)) * jnp.sqrt(1.0 - a / p)
    keep = jnp.sqrt(p) / jnp.sqrt(a)
    move = jnp.sqrt(1.0 - p - sigma * sigma) - keep * jnp.sqrt(1.0 - a)
    return keep, move, sigma


def silu(v):
    half = 0.5 * v
    return half + half * jnp.tanh(half)


def normalize(x):
    mean = jnp.sum(jnp.sum(x * x, axis=1, keepdims=True), axis=2, keepdims=True) * (1.0 / (C * NT))
    return x * lax.rsqrt(mean + 1e-05)


def block(rows, cond_rows, pairs, wide, wide_cond, wide_temporal):
    windows = [
        jnp.concatenate([row(2 * C * p, 2 * C * p + 4 * C) for row in rows], axis=0) for p in pairs
    ]
    fields = [cond_rows(p) for p in pairs]
    rhs = jnp.concatenate(windows, axis=1) if len(pairs) > 1 else windows[0]
    field = jnp.concatenate(fields, axis=1) if len(pairs) > 1 else fields[0]
    free = jnp.dot(wide[...], rhs, preferred_element_type=F32)
    given = (free + jnp.dot(wide_cond[...], field, preferred_element_type=F32)).astype(BF16)
    free = free.astype(BF16)
    hidden = (given + given * jnp.tanh(given)) * BF16(1.5) - (free + free * jnp.tanh(free))
    taps = jnp.dot(wide_temporal[...], hidden, preferred_element_type=F32)
    time = lax.broadcasted_iota(jnp.int32, (C, NT), 1)
    sums = []
    for q in range(len(pairs)):
        for o in range(2):
            t = taps[3 * C * o : 3 * C * (o + 1), NT * q : NT * (q + 1)]
            before = jnp.where(time == 0, 0.0, pltpu.roll(t[0:C], 1, 1))
            after = jnp.where(time == NT - 1, 0.0, pltpu.roll(t[2 * C :], NT - 1, 1))
            sums.append(before + t[C : 2 * C] + after)
    return sums


def prepare(x, fresh, factors):
    normed = normalize(x)
    act = silu(normed).astype(BF16).reshape(WIDE * C, NT)
    if fresh is None:
        return act, None
    keep, move, sigma = factors
    value = keep * x[1 : MID + 1] + move * normed[1 : MID + 1] + sigma * fresh
    return act, value.reshape(MID * C, NT)


def pick(ref, *lead):
    return lambda lo, hi: ref[(*lead, slice(lo, hi), slice(None))]


def first_step(rows, condx, e, base, move, weights):
    sums = block(
        rows, lambda p: condx[e, 2 * CK * p : 2 * CK * (p + 1), :], list(range(MID // 2)), *weights
    )
    for i, s in enumerate(sums):
        base[e, i * C : (i + 1) * C, :] = base[e, i * C : (i + 1) * C, :] + move * s


def inner_kernel(place, steps, lat, noise, cond, ya, yb, wide, wide_cond, wide_temporal, token, act, base, condx):
    del token
    factors = coefficients(steps[0], steps[1])
    lows, highs = halo_columns(place, ya, yb)
    for r in range(ROWS):
        low, high = lows(r), highs(r)
        act[r], base[r] = prepare(
            wide_latent(lat[r], low, high), wide_noise(noise[0, r], low, high), factors
        )
        condx[r] = wide_cond_row(cond[r], low, high)
    for r in range(1, ROWS - 1):
        first_step(
            [pick(act, r + d) for d in (-1, 0, 1)], condx, r, base, factors[1], (wide, wide_cond, wide_temporal)
        )


def inner(place, steps, lat, noise, cond, ya, yb, weights, token):
    return pl.pallas_call(
        inner_kernel,
        out_shape=(
            jax.ShapeDtypeStruct((ROWS, WIDE * C, NT), BF16),
            jax.ShapeDtypeStruct((ROWS, MID * C, NT), F32),
            jax.ShapeDtypeStruct((ROWS, MID * CK, NT), BF16),
        ),
        in_specs=[smem(), smem()] + [vmem()] * 9,
        out_specs=(vmem(),) * 3,
        compiler_params=pltpu.CompilerParams(vmem_limit_bytes=24 << 20),
        cost_estimate=pl.CostEstimate(flops=1 << 30, bytes_accessed=4 << 20, transcendentals=2 << 20),
        name="inner_rows",
    )(place, steps, lat, noise, cond, ya, yb, *weights, token)


def main_kernel(
    place, steps, noise, cond, xa, xb, act, base_own, condx_own, wide, wide_cond, wide_temporal,
    out, outer, base, condx, act2,
):
    weights = (wide, wide_cond, wide_temporal)
    factors = coefficients(steps[0], steps[1])
    even_x = place[0] == 0
    n = WIDE * C
    for top in (False, True):
        face = lambda lo, hi: jnp.where(even_x == top, xa[lo:hi, :], xb[lo:hi, :])
        near = 0 if top else 1
        for i in range(2):
            fresh = cells(face(2 * n, 2 * n + MID * C)) if i == near else None
            done, value = prepare(cells(face(i * n, (i + 1) * n)), fresh, factors)
            outer[2 * top + i] = done
            if i == near:
                base[2 + top] = value
                condx[2 + top] = face(2 * n + MID * C, XROWS)
    for i, r in enumerate((0, ROWS - 1)):
        base[i] = base_own[r]
        condx[i] = condx_own[r]

    halo = {-2: 0, -1: 1, ROWS: 2, ROWS + 1: 3}
    for r, slot in ((0, 0), (ROWS - 1, 1), (-1, 2), (ROWS, 3)):
        rows = [pick(outer, halo[r + d]) if r + d in halo else pick(act, r + d) for d in (-1, 0, 1)]
        first_step(rows, condx, slot, base, factors[1], weights)

    keep2, move2, sigma2 = coefficients(steps[1], steps[2])
    left = jnp.where(place[3] == 0, 0.0, 1.0)
    right = jnp.where(place[3] == NGY - 1, 0.0, 1.0)
    for e in range(6):
        r = e - 1
        x = (base_own[r] if 0 < r < ROWS - 1 else base[{0: 0, ROWS - 1: 1, -1: 2, ROWS: 3}[r]]).reshape(MID, C, NT)
        normed = normalize(x)
        value = silu(normed)
        value = jnp.concatenate([value[0:1] * left, value[1 : MID - 1], value[MID - 1 :] * right], axis=0)
        if e == 0:
            value = value * jnp.where(place[2] == 0, 0.0, 1.0)
        if e == 5:
            value = value * jnp.where(place[2] == NGX - 1, 0.0, 1.0)
        act2[e] = value.astype(BF16).reshape(MID * C, NT)
        if 0 < e < 5:
            out[r] = (
                keep2 * x[1 : MID - 1] + move2 * normed[1 : MID - 1] + sigma2 * noise[1, r].astype(F32)
            )

    def second(r, carry):
        sums = block(
            [pick(act2, r + d) for d in range(3)],
            lambda p: cond[r, 2 * CK * p : 2 * CK * (p + 1), :],
            list(range(COLS // 2)),
            *weights,
        )
        for i, s in enumerate(sums):
            out[r, i] = out[r, i] + move2 * s
        return carry

    lax.fori_loop(0, ROWS, second, 0)


def sample(place, steps, noise, cond, xa, xb, act, base, condx, weights):
    return pl.pallas_call(
        main_kernel,
        out_shape=jax.ShapeDtypeStruct((ROWS, COLS, C, NT), F32),
        in_specs=[smem(), smem()] + [vmem()] * 10,
        out_specs=vmem(),
        scratch_shapes=[
            pltpu.VMEM((4, WIDE * C, NT), BF16),
            pltpu.VMEM((4, MID * C, NT), F32),
            pltpu.VMEM((4, MID * CK, NT), BF16),
            pltpu.VMEM((6, MID * C, NT), BF16),
        ],
        compiler_params=pltpu.CompilerParams(vmem_limit_bytes=32 << 20),
        cost_estimate=pl.CostEstimate(flops=2 << 30, bytes_accessed=5 << 20, transcendentals=5 << 20),
        name="sample_slab",
    )(place, steps, noise, cond, xa, xb, act, base, condx, *weights)


def on_device(latent, sample_noise, cond_field, timesteps, spatial_weight, cond_weight, temporal_weight):
    gx, gy = lax.axis_index("gx"), lax.axis_index("gy")
    place = jnp.stack([gx % 2, gy % 2, gx, gy]).astype(jnp.int32)
    cond = cond_field.reshape(ROWS, COLS * CK, NT)
    ya, yb = pack_y(place, latent, sample_noise, cond)
    ya = lax.ppermute(ya, AXES, swaps_y(0))
    yb = lax.ppermute(yb, AXES, swaps_y(1))
    weights = widen(jnp.swapaxes(spatial_weight, 2, 3), cond_weight.T, temporal_weight)
    xa, xb, token = pack_x(place, latent, sample_noise, cond, ya, yb)
    xa = lax.ppermute(xa, AXES, swaps_x(0))
    xb = lax.ppermute(xb, AXES, swaps_x(1))
    act, base, condx = inner(place, timesteps, latent, sample_noise, cond, ya, yb, weights, token)
    return sample(place, timesteps, sample_noise, cond, xa, xb, act, base, condx, weights)


def solution(mesh):
    in_specs = (
        P("gx", "gy", None, None),
        P(None, "gx", "gy", None, None),
        P("gx", "gy", None, None),
        P(),
        P(),
        P(),
        P(),
    )
    return jax.shard_map(
        on_device, mesh=mesh, in_specs=in_specs, out_specs=P("gx", "gy", None, None), check_vma=False
    )
```

```python
import jax
import jax.numpy as jnp
from jax import lax
from jax.experimental import pallas as pl
from jax.experimental.pallas import tpu as pltpu
from jax.sharding import PartitionSpec as P

F32 = jnp.float32
BF16 = jnp.bfloat16
VMEM_ALL = 60 << 20
VMEM_MOST = 34 << 20
AXES = ("cfg", "gx", "gy")
NCFG, NGX, NGY = 2, 16, 8
ROWS, COLS, C, FF, CK, NT = 4, 16, 32, 128, 8, 128
YROWS = 2 * C + C + 2 * CK
WIDE, MID = COLS + 4, COLS + 2
XROWS = 2 * WIDE * C + MID * C + MID * CK


def linear(cfg, gx, gy):
    return (cfg * NGX + gx) * NGY + gy


def swaps_x(parity):
    pairs = []
    for cfg in range(NCFG):
        for gy in range(NGY):
            for gx in range(parity, NGX - 1, 2):
                other = 1 - cfg if gx == NGX // 2 - 1 else cfg
                a, b = linear(cfg, gx, gy), linear(other, gx + 1, gy)
                pairs += [(a, b), (b, a)]
    return pairs


def swaps_y(parity):
    pairs = []
    for cfg in range(NCFG):
        for gx in range(NGX):
            for gy in range(parity, NGY - 1, 2):
                a, b = linear(cfg, gx, gy), linear(cfg, gx, gy + 1)
                pairs += [(a, b), (b, a)]
    return pairs


def vmem():
    return pl.BlockSpec(memory_space=pltpu.VMEM)


def smem():
    return pl.BlockSpec(memory_space=pltpu.SMEM)


def join16(*parts):
    return jnp.concatenate([p.astype(F32) for p in parts], axis=0).astype(BF16)


def any_space():
    return pl.BlockSpec(memory_space=pl.ANY)


def cells(v):
    return v.astype(F32).reshape(-1, C, NT)


def pack_y_kernel(place, lat, noise, cond, ya, yb, token, xs, ns, cs, sems):
    token[...] = jnp.zeros(token.shape, F32)
    copies = []
    for side, (lo, inner, field) in enumerate(((0, 0, 0), (COLS - 2, COLS - 1, (COLS - 2) * CK))):
        copies.append(pltpu.make_async_copy(lat.at[:, lo : lo + 2], xs.at[side], sems.at[3 * side]))
        copies.append(pltpu.make_async_copy(noise.at[0, :, inner], ns.at[side], sems.at[3 * side + 1]))
        copies.append(
            pltpu.make_async_copy(cond.at[:, field : field + 2 * CK, :], cs.at[side], sems.at[3 * side + 2])
        )
    for copy in copies:
        copy.start()
    for copy in copies:
        copy.wait()

    def pack_y(out, side):
        for r in range(ROWS):
            out[r, 0 : 2 * C, :] = xs[side, r].reshape(2 * C, NT).astype(BF16)
            out[r, 2 * C : 3 * C, :] = ns[side, r]
            both = cs[side, r].astype(F32)
            cell = both[CK:] if side else both[0:CK]
            out[r, 3 * C :, :] = join16(cell, cell)

    for parity in range(2):

        @pl.when(place[1] == parity)
        def _():
            pack_y(ya, 1 - parity)
            pack_y(yb, parity)


def pack_y(place, lat, noise, cond):
    y = jax.ShapeDtypeStruct((ROWS, YROWS, NT), BF16)
    return pl.pallas_call(
        pack_y_kernel,
        out_shape=(y, y, jax.ShapeDtypeStruct((8, NT), F32)),
        in_specs=[smem(), any_space(), any_space(), any_space()],
        out_specs=(vmem(),) * 3,
        scratch_shapes=[
            pltpu.VMEM((2, ROWS, 2, C, NT), F32),
            pltpu.VMEM((2, ROWS, C, NT), BF16),
            pltpu.VMEM((2, ROWS, 2 * CK, NT), BF16),
            pltpu.SemaphoreType.DMA((6,)),
        ],
        compiler_params=pltpu.CompilerParams(vmem_limit_bytes=VMEM_ALL),
        cost_estimate=pl.CostEstimate(flops=1 << 16, bytes_accessed=1 << 19, transcendentals=0),
        name="pack_columns",
    )(place, lat, noise, cond)


def halo_columns(place, ya, yb):
    even = place[1] == 0
    return (
        lambda r: jnp.where(even, yb[r], ya[r]),
        lambda r: jnp.where(even, ya[r], yb[r]),
    )


def own_kernel(
    token, steps, lat, noise, act, base, packed, fresh, fresh2, xs, lat_sems, noise_sems, later_sem
):
    del token
    loads = []
    for r in range(ROWS):
        loads.append(
            (
                pltpu.make_async_copy(lat.at[r], xs.at[r], lat_sems.at[r]),
                pltpu.make_async_copy(noise.at[0, r], fresh.at[r], noise_sems.at[r]),
            )
        )
        for load in loads[-1]:
            load.start()
    later = pltpu.make_async_copy(noise.at[1], fresh2, later_sem)
    later.start()
    factors = coefficients(steps[0], steps[1])
    for r in range(ROWS):
        for load in loads[r]:
            load.wait()
        x = xs[r]
        packed[r] = x.astype(BF16).reshape(COLS * C, NT)
        act[r], base[r] = prepare(x, fresh[r], factors)
    later.wait()


def own(token, steps, lat, noise):
    n = COLS * C
    return pl.pallas_call(
        own_kernel,
        out_shape=(
            jax.ShapeDtypeStruct((ROWS, n, NT), BF16),
            jax.ShapeDtypeStruct((ROWS, n, NT), F32),
            jax.ShapeDtypeStruct((ROWS, n, NT), BF16),
            jax.ShapeDtypeStruct((ROWS, COLS, C, NT), BF16),
            jax.ShapeDtypeStruct((ROWS, COLS, C, NT), BF16),
        ),
        in_specs=[vmem(), smem(), any_space(), any_space()],
        out_specs=(vmem(),) * 5,
        scratch_shapes=[
            pltpu.VMEM((ROWS, COLS, C, NT), F32),
            pltpu.SemaphoreType.DMA((ROWS,)),
            pltpu.SemaphoreType.DMA((ROWS,)),
            pltpu.SemaphoreType.DMA,
        ],
        compiler_params=pltpu.CompilerParams(vmem_limit_bytes=VMEM_MOST),
        cost_estimate=pl.CostEstimate(flops=1 << 24, bytes_accessed=4 << 20, transcendentals=1 << 18),
        name="own_cells",
    )(token, steps, lat, noise)


def wide_cond_row(cond_row, low, high):
    return join16(low.astype(F32)[3 * C : 3 * C + CK], cond_row, high.astype(F32)[3 * C : 3 * C + CK])


def pack_x_kernel(place, packed, fresh, cond, ya, yb, xa, xb, token):
    lows, highs = halo_columns(place, ya, yb)

    def pack_x(out, top):
        lo, inner = (ROWS - 2, ROWS - 1) if top else (0, 0)
        n = WIDE * C
        for i in range(2):
            low, high = lows(lo + i), highs(lo + i)
            out[i * n : i * n + 2 * C, :] = low[0 : 2 * C]
            out[i * n + 2 * C : (i + 1) * n - 2 * C, :] = packed[lo + i]
            out[(i + 1) * n - 2 * C : (i + 1) * n, :] = high[0 : 2 * C]
            if lo + i == inner:
                at, end = 2 * n, 2 * n + MID * C
                out[at : at + C, :] = low[2 * C : 3 * C]
                out[at + C : end - C, :] = fresh[inner].reshape(COLS * C, NT)
                out[end - C : end, :] = high[2 * C : 3 * C]
                out[end:, :] = wide_cond_row(cond[inner], low, high)

    for parity in range(2):

        @pl.when(place[0] == parity)
        def _():
            pack_x(xa, parity == 0)
            pack_x(xb, parity == 1)

    token[...] = jnp.zeros(token.shape, F32)


def pack_x(place, packed, fresh, cond, ya, yb):
    x = jax.ShapeDtypeStruct((XROWS, NT), BF16)
    return pl.pallas_call(
        pack_x_kernel,
        out_shape=(x, x, jax.ShapeDtypeStruct((8, NT), F32)),
        in_specs=[smem()] + [vmem()] * 5,
        out_specs=(vmem(),) * 3,
        compiler_params=pltpu.CompilerParams(vmem_limit_bytes=24 << 20),
        cost_estimate=pl.CostEstimate(flops=1 << 18, bytes_accessed=3 << 20, transcendentals=0),
        name="pack_rows",
    )(place, packed, fresh, cond, ya, yb)


def weights_kernel(spatial, cond, temporal, wide, wide_cond, wide_temporal):
    blank = jnp.zeros((C, FF), F32)
    for dx in range(3):
        taps = [0.5 * spatial[dx, dy].astype(F32) for dy in range(3)]
        at = slice(dx * 4 * C, (dx + 1) * 4 * C)
        wide[0:FF, at] = jnp.concatenate(taps + [blank], axis=0).T.astype(BF16)
        wide[FF:, at] = jnp.concatenate([blank] + taps, axis=0).T.astype(BF16)
    small = 0.5 * cond[...].astype(F32)
    none = jnp.zeros((FF - CK, FF), F32)
    pair = jnp.concatenate([small, none], axis=0).T[:, 0:CK]
    gap = jnp.zeros((FF, CK), F32)
    wide_cond[0:FF, :] = jnp.concatenate([pair, gap], axis=1).astype(BF16)
    wide_cond[FF:, :] = jnp.concatenate([gap, pair], axis=1).astype(BF16)
    wide_temporal[...] = jnp.zeros(wide_temporal.shape, BF16)
    wide_temporal[0 : 3 * C, 0:FF] = (2.0 * temporal[...].astype(F32)).astype(BF16).reshape(3 * C, FF)
    wide_temporal[3 * C :, FF:] = (2.0 * temporal[...].astype(F32)).astype(BF16).reshape(3 * C, FF)


def widen(spatial, cond, temporal):
    return pl.pallas_call(
        weights_kernel,
        out_shape=(
            jax.ShapeDtypeStruct((2 * FF, 12 * C), BF16),
            jax.ShapeDtypeStruct((2 * FF, 2 * CK), BF16),
            jax.ShapeDtypeStruct((6 * C, 2 * FF), BF16),
        ),
        in_specs=[vmem()] * 3,
        out_specs=(vmem(),) * 3,
        compiler_params=pltpu.CompilerParams(vmem_limit_bytes=16 << 20),
        cost_estimate=pl.CostEstimate(flops=1 << 18, bytes_accessed=1 << 20, transcendentals=0),
        name="widen_weights",
    )(spatial, cond, temporal)


def log_alpha(when):
    shape = (8, 128)
    position = lax.broadcasted_iota(jnp.int32, shape, 0) * 128 + lax.broadcasted_iota(jnp.int32, shape, 1)
    beta = 0.0001 + (0.02 - 0.0001) * position.astype(F32) / 999.0
    logs = jnp.log(1.0 - jnp.minimum(beta, 0.5))
    return jnp.sum(jnp.where(position <= when, logs, 0.0))


def coefficients(now, later):
    a = jnp.exp(jnp.full((1, NT), log_alpha(now), F32))
    p = jnp.exp(jnp.full((1, NT), log_alpha(later), F32))
    sigma = 0.5 * jnp.sqrt((1.0 - p) / (1.0 - a)) * jnp.sqrt(1.0 - a / p)
    keep = jnp.sqrt(p) / jnp.sqrt(a)
    move = jnp.sqrt(1.0 - p - sigma * sigma) - keep * jnp.sqrt(1.0 - a)
    return keep, move, sigma


def silu(v):
    half = 0.5 * v
    return half + half * jnp.tanh(half)


def normalize(x):
    mean = jnp.sum(jnp.sum(x * x, axis=1, keepdims=True), axis=2, keepdims=True) * (1.0 / (C * NT))
    return x * lax.rsqrt(mean + 1e-05)


def spatial_sum(terms, pairs, wide):
    windows = [
        jnp.concatenate([row(2 * C * p, 2 * C * p + 4 * C) for _, row in terms], axis=0) for p in pairs
    ]
    taps = wide[:, 4 * C * terms[0][0] : 4 * C * (terms[-1][0] + 1)]
    return jnp.dot(taps, jnp.concatenate(windows, axis=1), preferred_element_type=F32)


def cond_pairs(term, first, pairs):
    cell = lambda i: term[:, NT * (first + i) : NT * (first + i + 1)]
    return jnp.concatenate(
        [jnp.concatenate([cell(2 * p), cell(2 * p + 1)], axis=0) for p in range(pairs)], axis=1
    )


def temporal_sum(free, given, wide_temporal):
    pairs = range(free.shape[1] // NT)
    given = given.astype(BF16)
    free = free.astype(BF16)
    hidden = (given + given * jnp.tanh(given)) * BF16(1.5) - (free + free * jnp.tanh(free))
    taps = jnp.dot(wide_temporal[...], hidden, preferred_element_type=F32)
    time = lax.broadcasted_iota(jnp.int32, (C, NT), 1)
    sums = []
    for q in pairs:
        for o in range(2):
            t = taps[3 * C * o : 3 * C * (o + 1), NT * q : NT * (q + 1)]
            before = jnp.where(time == 0, 0.0, pltpu.roll(t[0:C], 1, 1))
            after = jnp.where(time == NT - 1, 0.0, pltpu.roll(t[2 * C :], NT - 1, 1))
            sums.append(before + t[C : 2 * C] + after)
    return sums


def prepare(x, fresh, factors):
    normed = normalize(x)
    act = silu(normed).astype(BF16).reshape(-1, NT)
    if fresh is None:
        return act, None
    keep, move, sigma = factors
    skip = (x.shape[0] - fresh.shape[0]) // 2
    part = slice(skip, skip + fresh.shape[0])
    value = keep * x[part] + move * normed[part] + sigma * fresh.astype(F32)
    return act, value.reshape(-1, NT)


def pick(ref, *lead):
    return lambda lo, hi: ref[(*lead, slice(lo, hi), slice(None))]


def add_sums(sums, base, e, move):
    for i, s in enumerate(sums):
        base[e, i * C : (i + 1) * C, :] = base[e, i * C : (i + 1) * C, :] + move * s


FIRST = range(MID // 2)
SECOND = range(COLS // 2)


def next_act(value, row, place):
    left = jnp.where(place[3] == 0, 0.0, 1.0)
    right = jnp.where(place[3] == NGY - 1, 0.0, 1.0)
    value = jnp.concatenate([value[0:1] * left, value[1 : MID - 1], value[MID - 1 :] * right], axis=0)
    if row == -1:
        value = value * jnp.where(place[2] == 0, 0.0, 1.0)
    if row == ROWS:
        value = value * jnp.where(place[2] == NGX - 1, 0.0, 1.0)
    return value.astype(BF16).reshape(MID * C, NT)


def inner_kernel(
    place, steps, act_own, base_own, cond, ya, yb, wide, wide_cond, wide_temporal, token,
    act, base, term, part1, part2, act2,
):
    del token
    factors = coefficients(steps[0], steps[1])
    lows, highs = halo_columns(place, ya, yb)
    for r in range(ROWS):
        low, high = lows(r), highs(r)
        x = jnp.concatenate([cells(low[0 : 2 * C]), cells(high[0 : 2 * C])], axis=0)
        fresh = jnp.concatenate([cells(low[2 * C : 3 * C]), cells(high[2 * C : 3 * C])], axis=0)
        done, value = prepare(x, fresh, factors)
        act[r, 0 : 2 * C, :] = done[0 : 2 * C]
        act[r, 2 * C : (WIDE - 2) * C, :] = act_own[r]
        act[r, (WIDE - 2) * C :, :] = done[2 * C :]
        base[r, 0:C, :] = value[0:C]
        base[r, C : (MID - 1) * C, :] = base_own[r]
        base[r, (MID - 1) * C :, :] = value[C:]
        field = wide_cond_row(cond[r], low, high).astype(F32)
        field = jnp.concatenate([field[CK * i : CK * (i + 1)] for i in range(MID)], axis=1).astype(BF16)
        term[r] = jnp.dot(wide_cond[0:FF, 0:CK], field, preferred_element_type=F32)
    for r in range(1, ROWS - 1):
        free = spatial_sum([(d + 1, pick(act, r + d)) for d in (-1, 0, 1)], FIRST, wide)
        add_sums(
            temporal_sum(free, free + cond_pairs(term[r], 0, MID // 2), wide_temporal), base, r, factors[1]
        )
    part1[0] = spatial_sum([(1, pick(act, 0)), (2, pick(act, 1))], FIRST, wide)
    part1[1] = spatial_sum([(0, pick(act, ROWS - 2)), (1, pick(act, ROWS - 1))], FIRST, wide)
    part1[2] = spatial_sum([(2, pick(act, 0))], FIRST, wide)
    part1[3] = spatial_sum([(0, pick(act, ROWS - 1))], FIRST, wide)
    for i in range(2):
        act2[i] = next_act(silu(normalize(base[1 + i].reshape(MID, C, NT))), 1 + i, place)
    one, two = pick(act2, 0), pick(act2, 1)
    part2[0] = spatial_sum([(2, one)], SECOND, wide)
    part2[1] = spatial_sum([(1, one), (2, two)], SECOND, wide)
    part2[2] = spatial_sum([(0, one), (1, two)], SECOND, wide)
    part2[3] = spatial_sum([(0, two)], SECOND, wide)


def inner(place, steps, act, base, cond, ya, yb, weights, token):
    return pl.pallas_call(
        inner_kernel,
        out_shape=(
            jax.ShapeDtypeStruct((ROWS, WIDE * C, NT), BF16),
            jax.ShapeDtypeStruct((ROWS, MID * C, NT), F32),
            jax.ShapeDtypeStruct((ROWS, FF, MID * NT), F32),
            jax.ShapeDtypeStruct((4, 2 * FF, MID // 2 * NT), F32),
            jax.ShapeDtypeStruct((4, 2 * FF, COLS // 2 * NT), F32),
            jax.ShapeDtypeStruct((2, MID * C, NT), BF16),
        ),
        in_specs=[smem(), smem()] + [vmem()] * 9,
        out_specs=(vmem(),) * 6,
        compiler_params=pltpu.CompilerParams(vmem_limit_bytes=VMEM_MOST),
        cost_estimate=pl.CostEstimate(flops=1 << 30, bytes_accessed=4 << 20, transcendentals=2 << 20),
        name="inner_rows",
    )(place, steps, act, base, cond, ya, yb, *weights, token)


def main_kernel(
    place, steps, fresh2, xa, xb, act, base_own, term, part1, part2, act2_own, wide, wide_cond, wide_temporal,
    out, outer, base, act2,
):
    factors = coefficients(steps[0], steps[1])
    even_x = place[0] == 0
    n = WIDE * C
    fields = []
    for top in (False, True):
        face = lambda lo, hi: jnp.where(even_x == top, xa[lo:hi, :], xb[lo:hi, :])
        near = 0 if top else 1
        for i in range(2):
            fresh = cells(face(2 * n, 2 * n + MID * C)) if i == near else None
            done, value = prepare(cells(face(i * n, (i + 1) * n)), fresh, factors)
            outer[2 * top + i] = done
            if i == near:
                base[2 + top] = value
        fields.append(face(2 * n + MID * C, XROWS))
    for i, r in enumerate((0, ROWS - 1)):
        base[i] = base_own[r]

    far = (
        [(0, pick(outer, 1))],
        [(2, pick(outer, 2))],
        [(0, pick(outer, 0)), (1, pick(outer, 1))],
        [(1, pick(outer, 2)), (2, pick(outer, 3))],
    )
    for slot in range(4):
        free = part1[slot] + spatial_sum(far[slot], FIRST, wide)
        if slot < 2:
            given = free + cond_pairs(term[(ROWS - 1) * slot], 0, MID // 2)
        else:
            field = jnp.concatenate([fields[slot - 2][2 * CK * p : 2 * CK * (p + 1)] for p in FIRST], axis=1)
            given = free + jnp.dot(wide_cond[...], field, preferred_element_type=F32)
        add_sums(temporal_sum(free, given, wide_temporal), base, slot, factors[1])

    keep2, move2, sigma2 = coefficients(steps[1], steps[2])
    slots = {0: 0, ROWS - 1: 1, -1: 2, ROWS: 3}
    for r in range(-1, ROWS + 1):
        x = (base[slots[r]] if r in slots else base_own[r]).reshape(MID, C, NT)
        normed = normalize(x)
        if r in slots:
            act2[slots[r]] = next_act(silu(normed), r, place)
        if 0 <= r < ROWS:
            out[r] = (
                keep2 * x[1 : MID - 1] + move2 * normed[1 : MID - 1] + sigma2 * fresh2[r].astype(F32)
            )

    near = (
        [(0, pick(act2, 2)), (1, pick(act2, 0))],
        [(0, pick(act2, 0))],
        [(2, pick(act2, 1))],
        [(1, pick(act2, 1)), (2, pick(act2, 3))],
    )
    for r in range(ROWS):
        free = part2[r] + spatial_sum(near[r], SECOND, wide)
        sums = temporal_sum(free, free + cond_pairs(term[r], 1, COLS // 2), wide_temporal)
        for i, s in enumerate(sums):
            out[r, i] = out[r, i] + move2 * s


def sample(place, steps, fresh2, xa, xb, parts, weights):
    return pl.pallas_call(
        main_kernel,
        out_shape=jax.ShapeDtypeStruct((ROWS, COLS, C, NT), F32),
        in_specs=[smem(), smem()] + [vmem()] * 12,
        out_specs=vmem(),
        scratch_shapes=[
            pltpu.VMEM((4, WIDE * C, NT), BF16),
            pltpu.VMEM((4, MID * C, NT), F32),
            pltpu.VMEM((4, MID * C, NT), BF16),
        ],
        compiler_params=pltpu.CompilerParams(vmem_limit_bytes=VMEM_MOST),
        cost_estimate=pl.CostEstimate(flops=2 << 30, bytes_accessed=5 << 20, transcendentals=5 << 20),
        name="sample_slab",
    )(place, steps, fresh2, xa, xb, *parts, *weights)


def on_device(latent, sample_noise, cond_field, timesteps, spatial_weight, cond_weight, temporal_weight):
    gx, gy = lax.axis_index("gx"), lax.axis_index("gy")
    place = jnp.stack([gx % 2, gy % 2, gx, gy]).astype(jnp.int32)
    cond = cond_field.reshape(ROWS, COLS * CK, NT)
    ya, yb, token = pack_y(place, latent, sample_noise, cond)
    ya = lax.ppermute(ya, AXES, swaps_y(0))
    yb = lax.ppermute(yb, AXES, swaps_y(1))
    act, base, packed, fresh, fresh2 = own(token, timesteps, latent, sample_noise)
    weights = widen(jnp.swapaxes(spatial_weight, 2, 3), cond_weight.T, temporal_weight)
    xa, xb, token = pack_x(place, packed, fresh, cond, ya, yb)
    xa = lax.ppermute(xa, AXES, swaps_x(0))
    xb = lax.ppermute(xb, AXES, swaps_x(1))
    parts = inner(place, timesteps, act, base, cond, ya, yb, weights, token)
    return sample(place, timesteps, fresh2, xa, xb, parts, weights)


def solution(mesh):
    in_specs = (
        P("gx", "gy", None, None),
        P(None, "gx", "gy", None, None),
        P("gx", "gy", None, None),
        P(),
        P(),
        P(),
        P(),
    )
    return jax.shard_map(
        on_device, mesh=mesh, in_specs=in_specs, out_specs=P("gx", "gy", None, None), check_vma=False
    )
```

```python
import jax
import jax.numpy as jnp
from jax import lax
from jax.experimental import pallas as pl
from jax.experimental.pallas import tpu as pltpu
from jax.sharding import PartitionSpec as P

F32 = jnp.float32
BF16 = jnp.bfloat16
VMEM_ALL = 52 << 20
VMEM_MOST = 34 << 20
AXES = ("cfg", "gx", "gy")
NCFG, NGX, NGY = 2, 16, 8
ROWS, COLS, C, FF, CK, NT = 4, 16, 32, 128, 8, 128
YROWS = 2 * C + C + 2 * CK
WIDE, MID = COLS + 4, COLS + 2
XROWS = 2 * WIDE * C + MID * C + MID * CK


def linear(cfg, gx, gy):
    return (cfg * NGX + gx) * NGY + gy


def swaps_x(parity):
    pairs = []
    for cfg in range(NCFG):
        for gy in range(NGY):
            for gx in range(parity, NGX - 1, 2):
                other = 1 - cfg if gx == NGX // 2 - 1 else cfg
                a, b = linear(cfg, gx, gy), linear(other, gx + 1, gy)
                pairs += [(a, b), (b, a)]
    return pairs


def swaps_y(parity):
    pairs = []
    for cfg in range(NCFG):
        for gx in range(NGX):
            for gy in range(parity, NGY - 1, 2):
                a, b = linear(cfg, gx, gy), linear(cfg, gx, gy + 1)
                pairs += [(a, b), (b, a)]
    return pairs


def vmem():
    return pl.BlockSpec(memory_space=pltpu.VMEM)


def smem():
    return pl.BlockSpec(memory_space=pltpu.SMEM)


def join16(*parts):
    return jnp.concatenate([p.astype(F32) for p in parts], axis=0).astype(BF16)


def any_space():
    return pl.BlockSpec(memory_space=pl.ANY)


def cells(v):
    return v.astype(F32).reshape(-1, C, NT)


def pack_y_kernel(place, lat, noise, cond, ya, yb, token, xs, ns, cs, sems):
    token[...] = jnp.zeros(token.shape, F32)
    copies = []
    for side, (lo, inner, field) in enumerate(((0, 0, 0), (COLS - 2, COLS - 1, (COLS - 2) * CK))):
        copies.append(pltpu.make_async_copy(lat.at[:, lo : lo + 2], xs.at[side], sems.at[3 * side]))
        copies.append(pltpu.make_async_copy(noise.at[0, :, inner], ns.at[side], sems.at[3 * side + 1]))
        copies.append(
            pltpu.make_async_copy(cond.at[:, field : field + 2 * CK, :], cs.at[side], sems.at[3 * side + 2])
        )
    for copy in copies:
        copy.start()
    for copy in copies:
        copy.wait()

    def pack_y(out, side):
        for r in range(ROWS):
            out[r, 0 : 2 * C, :] = xs[side, r].reshape(2 * C, NT).astype(BF16)
            out[r, 2 * C : 3 * C, :] = ns[side, r]
            both = cs[side, r].astype(F32)
            cell = both[CK:] if side else both[0:CK]
            out[r, 3 * C :, :] = join16(cell, cell)

    for parity in range(2):

        @pl.when(place[1] == parity)
        def _():
            pack_y(ya, 1 - parity)
            pack_y(yb, parity)


def pack_y(place, lat, noise, cond):
    y = jax.ShapeDtypeStruct((ROWS, YROWS, NT), BF16)
    return pl.pallas_call(
        pack_y_kernel,
        out_shape=(y, y, jax.ShapeDtypeStruct((8, NT), F32)),
        in_specs=[smem(), any_space(), any_space(), any_space()],
        out_specs=(vmem(),) * 3,
        scratch_shapes=[
            pltpu.VMEM((2, ROWS, 2, C, NT), F32),
            pltpu.VMEM((2, ROWS, C, NT), BF16),
            pltpu.VMEM((2, ROWS, 2 * CK, NT), BF16),
            pltpu.SemaphoreType.DMA((6,)),
        ],
        compiler_params=pltpu.CompilerParams(vmem_limit_bytes=VMEM_ALL),
        cost_estimate=pl.CostEstimate(flops=1 << 16, bytes_accessed=1 << 19, transcendentals=0),
        name="pack_columns",
    )(place, lat, noise, cond)


def halo_columns(place, ya, yb):
    even = place[1] == 0
    return (
        lambda r: jnp.where(even, yb[r], ya[r]),
        lambda r: jnp.where(even, ya[r], yb[r]),
    )


def own_kernel(token, steps, lat, noise, act, base, packed):
    del token
    factors = coefficients(steps[0], steps[1])
    for r in range(ROWS):
        x = lat[r]
        packed[r] = x.astype(BF16).reshape(COLS * C, NT)
        act[r], base[r] = prepare(x, noise[0, r], factors)


def own(token, steps, lat, noise):
    n = COLS * C
    return pl.pallas_call(
        own_kernel,
        out_shape=(
            jax.ShapeDtypeStruct((ROWS, n, NT), BF16),
            jax.ShapeDtypeStruct((ROWS, n, NT), F32),
            jax.ShapeDtypeStruct((ROWS, n, NT), BF16),
        ),
        in_specs=[vmem(), smem(), vmem(), vmem()],
        out_specs=(vmem(),) * 3,
        compiler_params=pltpu.CompilerParams(vmem_limit_bytes=24 << 20),
        cost_estimate=pl.CostEstimate(flops=1 << 24, bytes_accessed=4 << 20, transcendentals=1 << 18),
        name="own_cells",
    )(token, steps, lat, noise)


def wide_cond_row(cond_row, low, high):
    return join16(low.astype(F32)[3 * C : 3 * C + CK], cond_row, high.astype(F32)[3 * C : 3 * C + CK])


def pack_x_kernel(place, packed, noise, cond, ya, yb, xa, xb, token):
    lows, highs = halo_columns(place, ya, yb)

    def pack_x(out, top):
        lo, inner = (ROWS - 2, ROWS - 1) if top else (0, 0)
        n = WIDE * C
        for i in range(2):
            low, high = lows(lo + i), highs(lo + i)
            out[i * n : i * n + 2 * C, :] = low[0 : 2 * C]
            out[i * n + 2 * C : (i + 1) * n - 2 * C, :] = packed[lo + i]
            out[(i + 1) * n - 2 * C : (i + 1) * n, :] = high[0 : 2 * C]
            if lo + i == inner:
                at, end = 2 * n, 2 * n + MID * C
                out[at : at + C, :] = low[2 * C : 3 * C]
                out[at + C : end - C, :] = noise[0, inner].reshape(COLS * C, NT)
                out[end - C : end, :] = high[2 * C : 3 * C]
                out[end:, :] = wide_cond_row(cond[inner], low, high)

    for parity in range(2):

        @pl.when(place[0] == parity)
        def _():
            pack_x(xa, parity == 0)
            pack_x(xb, parity == 1)

    token[...] = jnp.zeros(token.shape, F32)


def pack_x(place, packed, noise, cond, ya, yb):
    x = jax.ShapeDtypeStruct((XROWS, NT), BF16)
    return pl.pallas_call(
        pack_x_kernel,
        out_shape=(x, x, jax.ShapeDtypeStruct((8, NT), F32)),
        in_specs=[smem()] + [vmem()] * 5,
        out_specs=(vmem(),) * 3,
        compiler_params=pltpu.CompilerParams(vmem_limit_bytes=24 << 20),
        cost_estimate=pl.CostEstimate(flops=1 << 18, bytes_accessed=3 << 20, transcendentals=0),
        name="pack_rows",
    )(place, packed, noise, cond, ya, yb)


def weights_kernel(spatial, cond, temporal, wide, wide_cond, wide_temporal):
    blank = jnp.zeros((C, FF), F32)
    for dx in range(3):
        taps = [0.5 * spatial[dx, dy].astype(F32) for dy in range(3)]
        at = slice(dx * 4 * C, (dx + 1) * 4 * C)
        wide[0:FF, at] = jnp.concatenate(taps + [blank], axis=0).T.astype(BF16)
        wide[FF:, at] = jnp.concatenate([blank] + taps, axis=0).T.astype(BF16)
    small = 0.5 * cond[...].astype(F32)
    none = jnp.zeros((FF - CK, FF), F32)
    pair = jnp.concatenate([small, none], axis=0).T[:, 0:CK]
    gap = jnp.zeros((FF, CK), F32)
    wide_cond[0:FF, :] = jnp.concatenate([pair, gap], axis=1).astype(BF16)
    wide_cond[FF:, :] = jnp.concatenate([gap, pair], axis=1).astype(BF16)
    wide_temporal[...] = jnp.zeros(wide_temporal.shape, BF16)
    wide_temporal[0 : 3 * C, 0:FF] = (2.0 * temporal[...].astype(F32)).astype(BF16).reshape(3 * C, FF)
    wide_temporal[3 * C :, FF:] = (2.0 * temporal[...].astype(F32)).astype(BF16).reshape(3 * C, FF)


def widen(spatial, cond, temporal):
    return pl.pallas_call(
        weights_kernel,
        out_shape=(
            jax.ShapeDtypeStruct((2 * FF, 12 * C), BF16),
            jax.ShapeDtypeStruct((2 * FF, 2 * CK), BF16),
            jax.ShapeDtypeStruct((6 * C, 2 * FF), BF16),
        ),
        in_specs=[vmem()] * 3,
        out_specs=(vmem(),) * 3,
        compiler_params=pltpu.CompilerParams(vmem_limit_bytes=16 << 20),
        cost_estimate=pl.CostEstimate(flops=1 << 18, bytes_accessed=1 << 20, transcendentals=0),
        name="widen_weights",
    )(spatial, cond, temporal)


def log_alpha(when):
    shape = (8, 128)
    position = lax.broadcasted_iota(jnp.int32, shape, 0) * 128 + lax.broadcasted_iota(jnp.int32, shape, 1)
    beta = 0.0001 + (0.02 - 0.0001) * position.astype(F32) / 999.0
    logs = jnp.log(1.0 - jnp.minimum(beta, 0.5))
    return jnp.sum(jnp.where(position <= when, logs, 0.0))


def coefficients(now, later):
    a = jnp.exp(jnp.full((1, NT), log_alpha(now), F32))
    p = jnp.exp(jnp.full((1, NT), log_alpha(later), F32))
    sigma = 0.5 * jnp.sqrt((1.0 - p) / (1.0 - a)) * jnp.sqrt(1.0 - a / p)
    keep = jnp.sqrt(p) / jnp.sqrt(a)
    move = jnp.sqrt(1.0 - p - sigma * sigma) - keep * jnp.sqrt(1.0 - a)
    return keep, move, sigma


def silu(v):
    half = 0.5 * v
    return half + half * jnp.tanh(half)


def normalize(x):
    mean = jnp.sum(jnp.sum(x * x, axis=1, keepdims=True), axis=2, keepdims=True) * (1.0 / (C * NT))
    return x * lax.rsqrt(mean + 1e-05)


def spatial_sum(terms, pairs, wide):
    windows = [
        jnp.concatenate([row(2 * C * p, 2 * C * p + 4 * C) for _, row in terms], axis=0) for p in pairs
    ]
    taps = wide[:, 4 * C * terms[0][0] : 4 * C * (terms[-1][0] + 1)]
    return jnp.dot(taps, jnp.concatenate(windows, axis=1), preferred_element_type=F32)


def cond_pairs(term, first, pairs):
    cell = lambda i: term[:, NT * (first + i) : NT * (first + i + 1)]
    return jnp.concatenate(
        [jnp.concatenate([cell(2 * p), cell(2 * p + 1)], axis=0) for p in range(pairs)], axis=1
    )


def temporal_sum(free, given, wide_temporal):
    pairs = range(free.shape[1] // NT)
    given = given.astype(BF16)
    free = free.astype(BF16)
    hidden = (given + given * jnp.tanh(given)) * BF16(1.5) - (free + free * jnp.tanh(free))
    taps = jnp.dot(wide_temporal[...], hidden, preferred_element_type=F32)
    time = lax.broadcasted_iota(jnp.int32, (C, NT), 1)
    sums = []
    for q in pairs:
        for o in range(2):
            t = taps[3 * C * o : 3 * C * (o + 1), NT * q : NT * (q + 1)]
            before = jnp.where(time == 0, 0.0, pltpu.roll(t[0:C], 1, 1))
            after = jnp.where(time == NT - 1, 0.0, pltpu.roll(t[2 * C :], NT - 1, 1))
            sums.append(before + t[C : 2 * C] + after)
    return sums


def prepare(x, fresh, factors):
    normed = normalize(x)
    act = silu(normed).astype(BF16).reshape(-1, NT)
    if fresh is None:
        return act, None
    keep, move, sigma = factors
    skip = (x.shape[0] - fresh.shape[0]) // 2
    part = slice(skip, skip + fresh.shape[0])
    value = keep * x[part] + move * normed[part] + sigma * fresh.astype(F32)
    return act, value.reshape(-1, NT)


def pick(ref, *lead):
    return lambda lo, hi: ref[(*lead, slice(lo, hi), slice(None))]


def add_sums(sums, base, e, move):
    for i, s in enumerate(sums):
        base[e, i * C : (i + 1) * C, :] = base[e, i * C : (i + 1) * C, :] + move * s


FIRST = range(MID // 2)
SECOND = range(COLS // 2)


def next_act(value, row, place):
    left = jnp.where(place[3] == 0, 0.0, 1.0)
    right = jnp.where(place[3] == NGY - 1, 0.0, 1.0)
    value = jnp.concatenate([value[0:1] * left, value[1 : MID - 1], value[MID - 1 :] * right], axis=0)
    if row == -1:
        value = value * jnp.where(place[2] == 0, 0.0, 1.0)
    if row == ROWS:
        value = value * jnp.where(place[2] == NGX - 1, 0.0, 1.0)
    return value.astype(BF16).reshape(MID * C, NT)


def inner_kernel(
    place, steps, act_own, base_own, cond, ya, yb, wide, wide_cond, wide_temporal, token,
    act, base, term, part1, part2, act2,
):
    del token
    factors = coefficients(steps[0], steps[1])
    lows, highs = halo_columns(place, ya, yb)
    for r in range(ROWS):
        low, high = lows(r), highs(r)
        x = jnp.concatenate([cells(low[0 : 2 * C]), cells(high[0 : 2 * C])], axis=0)
        fresh = jnp.concatenate([cells(low[2 * C : 3 * C]), cells(high[2 * C : 3 * C])], axis=0)
        done, value = prepare(x, fresh, factors)
        act[r, 0 : 2 * C, :] = done[0 : 2 * C]
        act[r, 2 * C : (WIDE - 2) * C, :] = act_own[r]
        act[r, (WIDE - 2) * C :, :] = done[2 * C :]
        base[r, 0:C, :] = value[0:C]
        base[r, C : (MID - 1) * C, :] = base_own[r]
        base[r, (MID - 1) * C :, :] = value[C:]
        field = wide_cond_row(cond[r], low, high).astype(F32)
        field = jnp.concatenate([field[CK * i : CK * (i + 1)] for i in range(MID)], axis=1).astype(BF16)
        term[r] = jnp.dot(wide_cond[0:FF, 0:CK], field, preferred_element_type=F32)
    for r in range(1, ROWS - 1):
        free = spatial_sum([(d + 1, pick(act, r + d)) for d in (-1, 0, 1)], FIRST, wide)
        add_sums(
            temporal_sum(free, free + cond_pairs(term[r], 0, MID // 2), wide_temporal), base, r, factors[1]
        )
    part1[0] = spatial_sum([(1, pick(act, 0)), (2, pick(act, 1))], FIRST, wide)
    part1[1] = spatial_sum([(0, pick(act, ROWS - 2)), (1, pick(act, ROWS - 1))], FIRST, wide)
    part1[2] = spatial_sum([(2, pick(act, 0))], FIRST, wide)
    part1[3] = spatial_sum([(0, pick(act, ROWS - 1))], FIRST, wide)
    for i in range(2):
        act2[i] = next_act(silu(normalize(base[1 + i].reshape(MID, C, NT))), 1 + i, place)
    one, two = pick(act2, 0), pick(act2, 1)
    part2[0] = spatial_sum([(2, one)], SECOND, wide)
    part2[1] = spatial_sum([(1, one), (2, two)], SECOND, wide)
    part2[2] = spatial_sum([(0, one), (1, two)], SECOND, wide)
    part2[3] = spatial_sum([(0, two)], SECOND, wide)


def inner(place, steps, act, base, cond, ya, yb, weights, token):
    return pl.pallas_call(
        inner_kernel,
        out_shape=(
            jax.ShapeDtypeStruct((ROWS, WIDE * C, NT), BF16),
            jax.ShapeDtypeStruct((ROWS, MID * C, NT), F32),
            jax.ShapeDtypeStruct((ROWS, FF, MID * NT), F32),
            jax.ShapeDtypeStruct((4, 2 * FF, MID // 2 * NT), F32),
            jax.ShapeDtypeStruct((4, 2 * FF, COLS // 2 * NT), F32),
            jax.ShapeDtypeStruct((2, MID * C, NT), BF16),
        ),
        in_specs=[smem(), smem()] + [vmem()] * 9,
        out_specs=(vmem(),) * 6,
        compiler_params=pltpu.CompilerParams(vmem_limit_bytes=VMEM_MOST),
        cost_estimate=pl.CostEstimate(flops=1 << 30, bytes_accessed=4 << 20, transcendentals=2 << 20),
        name="inner_rows",
    )(place, steps, act, base, cond, ya, yb, *weights, token)


def main_kernel(
    place, steps, noise, xa, xb, act, base_own, term, part1, part2, act2_own, wide, wide_cond, wide_temporal,
    out, outer, base, act2,
):
    factors = coefficients(steps[0], steps[1])
    even_x = place[0] == 0
    n = WIDE * C
    fields = []
    for top in (False, True):
        face = lambda lo, hi: jnp.where(even_x == top, xa[lo:hi, :], xb[lo:hi, :])
        near = 0 if top else 1
        for i in range(2):
            fresh = cells(face(2 * n, 2 * n + MID * C)) if i == near else None
            done, value = prepare(cells(face(i * n, (i + 1) * n)), fresh, factors)
            outer[2 * top + i] = done
            if i == near:
                base[2 + top] = value
        fields.append(face(2 * n + MID * C, XROWS))
    for i, r in enumerate((0, ROWS - 1)):
        base[i] = base_own[r]

    far = (
        [(0, pick(outer, 1))],
        [(2, pick(outer, 2))],
        [(0, pick(outer, 0)), (1, pick(outer, 1))],
        [(1, pick(outer, 2)), (2, pick(outer, 3))],
    )
    for slot in range(4):
        free = part1[slot] + spatial_sum(far[slot], FIRST, wide)
        if slot < 2:
            given = free + cond_pairs(term[(ROWS - 1) * slot], 0, MID // 2)
        else:
            field = jnp.concatenate([fields[slot - 2][2 * CK * p : 2 * CK * (p + 1)] for p in FIRST], axis=1)
            given = free + jnp.dot(wide_cond[...], field, preferred_element_type=F32)
        add_sums(temporal_sum(free, given, wide_temporal), base, slot, factors[1])

    keep2, move2, sigma2 = coefficients(steps[1], steps[2])
    slots = {0: 0, ROWS - 1: 1, -1: 2, ROWS: 3}
    for r in range(-1, ROWS + 1):
        x = (base[slots[r]] if r in slots else base_own[r]).reshape(MID, C, NT)
        normed = normalize(x)
        if r in slots:
            act2[slots[r]] = next_act(silu(normed), r, place)
        if 0 <= r < ROWS:
            out[r] = (
                keep2 * x[1 : MID - 1] + move2 * normed[1 : MID - 1] + sigma2 * noise[1, r].astype(F32)
            )

    near = (
        [(0, pick(act2, 2)), (1, pick(act2, 0))],
        [(0, pick(act2, 0))],
        [(2, pick(act2, 1))],
        [(1, pick(act2, 1)), (2, pick(act2, 3))],
    )
    for r in range(ROWS):
        free = part2[r] + spatial_sum(near[r], SECOND, wide)
        sums = temporal_sum(free, free + cond_pairs(term[r], 1, COLS // 2), wide_temporal)
        for i, s in enumerate(sums):
            out[r, i] = out[r, i] + move2 * s


def sample(place, steps, noise, xa, xb, parts, weights):
    return pl.pallas_call(
        main_kernel,
        out_shape=jax.ShapeDtypeStruct((ROWS, COLS, C, NT), F32),
        in_specs=[smem(), smem()] + [vmem()] * 12,
        out_specs=vmem(),
        scratch_shapes=[
            pltpu.VMEM((4, WIDE * C, NT), BF16),
            pltpu.VMEM((4, MID * C, NT), F32),
            pltpu.VMEM((4, MID * C, NT), BF16),
        ],
        compiler_params=pltpu.CompilerParams(vmem_limit_bytes=VMEM_MOST),
        cost_estimate=pl.CostEstimate(flops=2 << 30, bytes_accessed=5 << 20, transcendentals=5 << 20),
        name="sample_slab",
    )(place, steps, noise, xa, xb, *parts, *weights)


def on_device(latent, sample_noise, cond_field, timesteps, spatial_weight, cond_weight, temporal_weight):
    gx, gy = lax.axis_index("gx"), lax.axis_index("gy")
    place = jnp.stack([gx % 2, gy % 2, gx, gy]).astype(jnp.int32)
    cond = cond_field.reshape(ROWS, COLS * CK, NT)
    ya, yb, token = pack_y(place, latent, sample_noise, cond)
    ya = lax.ppermute(ya, AXES, swaps_y(0))
    yb = lax.ppermute(yb, AXES, swaps_y(1))
    act, base, packed = own(token, timesteps, latent, sample_noise)
    weights = widen(jnp.swapaxes(spatial_weight, 2, 3), cond_weight.T, temporal_weight)
    xa, xb, token = pack_x(place, packed, sample_noise, cond, ya, yb)
    xa = lax.ppermute(xa, AXES, swaps_x(0))
    xb = lax.ppermute(xb, AXES, swaps_x(1))
    parts = inner(place, timesteps, act, base, cond, ya, yb, weights, token)
    return sample(place, timesteps, sample_noise, xa, xb, parts, weights)


def solution(mesh):
    in_specs = (
        P("gx", "gy", None, None),
        P(None, "gx", "gy", None, None),
        P("gx", "gy", None, None),
        P(),
        P(),
        P(),
        P(),
    )
    return jax.shard_map(
        on_device, mesh=mesh, in_specs=in_specs, out_specs=P("gx", "gy", None, None), check_vma=False
    )
```

```python
import jax
import jax.numpy as jnp
from jax import lax
from jax.experimental import pallas as pl
from jax.experimental.pallas import tpu as pltpu
from jax.sharding import PartitionSpec as P

F32 = jnp.float32
BF16 = jnp.bfloat16
VMEM_ALL = 52 << 20
VMEM_MOST = 34 << 20
AXES = ("cfg", "gx", "gy")
NCFG, NGX, NGY = 2, 16, 8
ROWS, COLS, C, FF, CK, NT = 4, 16, 32, 128, 8, 128
YROWS = 2 * C + C + 2 * CK
WIDE, MID = COLS + 4, COLS + 2
XROWS = 2 * WIDE * C + MID * C + MID * CK


def linear(cfg, gx, gy):
    return (cfg * NGX + gx) * NGY + gy


def swaps_x(parity):
    pairs = []
    for cfg in range(NCFG):
        for gy in range(NGY):
            for gx in range(parity, NGX - 1, 2):
                other = 1 - cfg if gx == NGX // 2 - 1 else cfg
                a, b = linear(cfg, gx, gy), linear(other, gx + 1, gy)
                pairs += [(a, b), (b, a)]
    return pairs


def swaps_y(parity):
    pairs = []
    for cfg in range(NCFG):
        for gx in range(NGX):
            for gy in range(parity, NGY - 1, 2):
                a, b = linear(cfg, gx, gy), linear(cfg, gx, gy + 1)
                pairs += [(a, b), (b, a)]
    return pairs


def vmem():
    return pl.BlockSpec(memory_space=pltpu.VMEM)


def smem():
    return pl.BlockSpec(memory_space=pltpu.SMEM)


def join16(*parts):
    return jnp.concatenate([p.astype(F32) for p in parts], axis=0).astype(BF16)


def any_space():
    return pl.BlockSpec(memory_space=pl.ANY)


def cells(v):
    return v.astype(F32).reshape(-1, C, NT)


def pack_y_kernel(place, lat, noise, cond, ya, yb, token, xs, ns, cs, sems):
    token[...] = jnp.zeros(token.shape, F32)
    copies = []
    for side, (lo, inner, field) in enumerate(((0, 0, 0), (COLS - 2, COLS - 1, (COLS - 2) * CK))):
        copies.append(pltpu.make_async_copy(lat.at[:, lo : lo + 2], xs.at[side], sems.at[3 * side]))
        copies.append(pltpu.make_async_copy(noise.at[0, :, inner], ns.at[side], sems.at[3 * side + 1]))
        copies.append(
            pltpu.make_async_copy(cond.at[:, field : field + 2 * CK, :], cs.at[side], sems.at[3 * side + 2])
        )
    for copy in copies:
        copy.start()
    for copy in copies:
        copy.wait()

    def pack_y(out, side):
        for r in range(ROWS):
            out[r, 0 : 2 * C, :] = xs[side, r].reshape(2 * C, NT).astype(BF16)
            out[r, 2 * C : 3 * C, :] = ns[side, r]
            both = cs[side, r].astype(F32)
            cell = both[CK:] if side else both[0:CK]
            out[r, 3 * C :, :] = join16(cell, cell)

    for parity in range(2):

        @pl.when(place[1] == parity)
        def _():
            pack_y(ya, 1 - parity)
            pack_y(yb, parity)


def pack_y(place, lat, noise, cond):
    y = jax.ShapeDtypeStruct((ROWS, YROWS, NT), BF16)
    return pl.pallas_call(
        pack_y_kernel,
        out_shape=(y, y, jax.ShapeDtypeStruct((8, NT), F32)),
        in_specs=[smem(), any_space(), any_space(), any_space()],
        out_specs=(vmem(),) * 3,
        scratch_shapes=[
            pltpu.VMEM((2, ROWS, 2, C, NT), F32),
            pltpu.VMEM((2, ROWS, C, NT), BF16),
            pltpu.VMEM((2, ROWS, 2 * CK, NT), BF16),
            pltpu.SemaphoreType.DMA((6,)),
        ],
        compiler_params=pltpu.CompilerParams(vmem_limit_bytes=VMEM_ALL),
        cost_estimate=pl.CostEstimate(flops=1 << 16, bytes_accessed=1 << 19, transcendentals=0),
        name="pack_columns",
    )(place, lat, noise, cond)


def halo_columns(place, ya, yb):
    even = place[1] == 0
    return (
        lambda r: jnp.where(even, yb[r], ya[r]),
        lambda r: jnp.where(even, ya[r], yb[r]),
    )


def own_kernel(token, steps, lat, noise, act, base, packed):
    del token
    factors = coefficients(steps[0], steps[1])
    for r in range(ROWS):
        x = lat[r]
        packed[r] = x.astype(BF16).reshape(COLS * C, NT)
        act[r], base[r] = prepare(x, noise[0, r], factors)


def own(token, steps, lat, noise):
    n = COLS * C
    return pl.pallas_call(
        own_kernel,
        out_shape=(
            jax.ShapeDtypeStruct((ROWS, n, NT), BF16),
            jax.ShapeDtypeStruct((ROWS, n, NT), F32),
            jax.ShapeDtypeStruct((ROWS, n, NT), BF16),
        ),
        in_specs=[vmem(), smem(), vmem(), vmem()],
        out_specs=(vmem(),) * 3,
        compiler_params=pltpu.CompilerParams(vmem_limit_bytes=24 << 20),
        cost_estimate=pl.CostEstimate(flops=1 << 24, bytes_accessed=4 << 20, transcendentals=1 << 18),
        name="own_cells",
    )(token, steps, lat, noise)


def wide_cond_row(cond_row, low, high):
    return join16(low.astype(F32)[3 * C : 3 * C + CK], cond_row, high.astype(F32)[3 * C : 3 * C + CK])


def pack_x_kernel(place, packed, noise, cond, ya, yb, xb, xa, token):
    lows, highs = halo_columns(place, ya, yb)

    def pack_x(out, top):
        lo, inner = (ROWS - 2, ROWS - 1) if top else (0, 0)
        n = WIDE * C
        for i in range(2):
            low, high = lows(lo + i), highs(lo + i)
            out[i * n : i * n + 2 * C, :] = low[0 : 2 * C]
            out[i * n + 2 * C : (i + 1) * n - 2 * C, :] = packed[lo + i]
            out[(i + 1) * n - 2 * C : (i + 1) * n, :] = high[0 : 2 * C]
            if lo + i == inner:
                at, end = 2 * n, 2 * n + MID * C
                out[at : at + C, :] = low[2 * C : 3 * C]
                out[at + C : end - C, :] = noise[0, inner].reshape(COLS * C, NT)
                out[end - C : end, :] = high[2 * C : 3 * C]
                out[end:, :] = wide_cond_row(cond[inner], low, high)

    for parity in range(2):

        @pl.when(place[0] == parity)
        def _():
            pack_x(xa, parity == 0)
            pack_x(xb, parity == 1)

    token[...] = jnp.zeros(token.shape, F32)


def pack_x(place, packed, noise, cond, ya, yb):
    x = jax.ShapeDtypeStruct((XROWS, NT), BF16)
    return pl.pallas_call(
        pack_x_kernel,
        out_shape=(x, x, jax.ShapeDtypeStruct((8, NT), F32)),
        in_specs=[smem()] + [vmem()] * 5,
        out_specs=(vmem(),) * 3,
        compiler_params=pltpu.CompilerParams(vmem_limit_bytes=24 << 20),
        cost_estimate=pl.CostEstimate(flops=1 << 18, bytes_accessed=3 << 20, transcendentals=0),
        name="pack_rows",
    )(place, packed, noise, cond, ya, yb)


def weights_kernel(spatial, cond, temporal, wide, wide_cond, wide_temporal):
    blank = jnp.zeros((C, FF), F32)
    for dx in range(3):
        taps = [0.5 * spatial[dx, dy].astype(F32) for dy in range(3)]
        at = slice(dx * 4 * C, (dx + 1) * 4 * C)
        wide[0:FF, at] = jnp.concatenate(taps + [blank], axis=0).T.astype(BF16)
        wide[FF:, at] = jnp.concatenate([blank] + taps, axis=0).T.astype(BF16)
    small = 0.5 * cond[...].astype(F32)
    none = jnp.zeros((FF - CK, FF), F32)
    pair = jnp.concatenate([small, none], axis=0).T[:, 0:CK]
    gap = jnp.zeros((FF, CK), F32)
    wide_cond[0:FF, :] = jnp.concatenate([pair, gap], axis=1).astype(BF16)
    wide_cond[FF:, :] = jnp.concatenate([gap, pair], axis=1).astype(BF16)
    wide_temporal[...] = jnp.zeros(wide_temporal.shape, BF16)
    wide_temporal[0 : 3 * C, 0:FF] = (2.0 * temporal[...].astype(F32)).astype(BF16).reshape(3 * C, FF)
    wide_temporal[3 * C :, FF:] = (2.0 * temporal[...].astype(F32)).astype(BF16).reshape(3 * C, FF)


def widen(spatial, cond, temporal):
    return pl.pallas_call(
        weights_kernel,
        out_shape=(
            jax.ShapeDtypeStruct((2 * FF, 12 * C), BF16),
            jax.ShapeDtypeStruct((2 * FF, 2 * CK), BF16),
            jax.ShapeDtypeStruct((6 * C, 2 * FF), BF16),
        ),
        in_specs=[vmem()] * 3,
        out_specs=(vmem(),) * 3,
        compiler_params=pltpu.CompilerParams(vmem_limit_bytes=16 << 20),
        cost_estimate=pl.CostEstimate(flops=1 << 18, bytes_accessed=1 << 20, transcendentals=0),
        name="widen_weights",
    )(spatial, cond, temporal)


def log_alpha(when):
    shape = (8, 128)
    position = lax.broadcasted_iota(jnp.int32, shape, 0) * 128 + lax.broadcasted_iota(jnp.int32, shape, 1)
    beta = 0.0001 + (0.02 - 0.0001) * position.astype(F32) / 999.0
    logs = jnp.log(1.0 - jnp.minimum(beta, 0.5))
    return jnp.sum(jnp.where(position <= when, logs, 0.0))


def coefficients(now, later):
    a = jnp.exp(jnp.full((1, NT), log_alpha(now), F32))
    p = jnp.exp(jnp.full((1, NT), log_alpha(later), F32))
    sigma = 0.5 * jnp.sqrt((1.0 - p) / (1.0 - a)) * jnp.sqrt(1.0 - a / p)
    keep = jnp.sqrt(p) / jnp.sqrt(a)
    move = jnp.sqrt(1.0 - p - sigma * sigma) - keep * jnp.sqrt(1.0 - a)
    return keep, move, sigma


def silu(v):
    half = 0.5 * v
    return half + half * jnp.tanh(half)


def normalize(x):
    mean = jnp.sum(jnp.sum(x * x, axis=1, keepdims=True), axis=2, keepdims=True) * (1.0 / (C * NT))
    return x * lax.rsqrt(mean + 1e-05)


def spatial_sum(terms, pairs, wide):
    windows = [
        jnp.concatenate([row(2 * C * p, 2 * C * p + 4 * C) for _, row in terms], axis=0) for p in pairs
    ]
    taps = wide[:, 4 * C * terms[0][0] : 4 * C * (terms[-1][0] + 1)]
    return jnp.dot(taps, jnp.concatenate(windows, axis=1), preferred_element_type=F32)


def cond_pairs(term, first, pairs):
    cell = lambda i: term[:, NT * (first + i) : NT * (first + i + 1)]
    return jnp.concatenate(
        [jnp.concatenate([cell(2 * p), cell(2 * p + 1)], axis=0) for p in range(pairs)], axis=1
    )


def temporal_sum(free, given, wide_temporal):
    pairs = range(free.shape[1] // NT)
    given = given.astype(BF16)
    free = free.astype(BF16)
    hidden = (given + given * jnp.tanh(given)) * BF16(1.5) - (free + free * jnp.tanh(free))
    taps = jnp.dot(wide_temporal[...], hidden, preferred_element_type=F32)
    time = lax.broadcasted_iota(jnp.int32, (C, NT), 1)
    sums = []
    for q in pairs:
        for o in range(2):
            t = taps[3 * C * o : 3 * C * (o + 1), NT * q : NT * (q + 1)]
            before = jnp.where(time == 0, 0.0, pltpu.roll(t[0:C], 1, 1))
            after = jnp.where(time == NT - 1, 0.0, pltpu.roll(t[2 * C :], NT - 1, 1))
            sums.append(before + t[C : 2 * C] + after)
    return sums


def prepare(x, fresh, factors):
    normed = normalize(x)
    act = silu(normed).astype(BF16).reshape(-1, NT)
    if fresh is None:
        return act, None
    keep, move, sigma = factors
    skip = (x.shape[0] - fresh.shape[0]) // 2
    part = slice(skip, skip + fresh.shape[0])
    value = keep * x[part] + move * normed[part] + sigma * fresh.astype(F32)
    return act, value.reshape(-1, NT)


def pick(ref, *lead):
    return lambda lo, hi: ref[(*lead, slice(lo, hi), slice(None))]


def add_sums(sums, base, e, move):
    for i, s in enumerate(sums):
        base[e, i * C : (i + 1) * C, :] = base[e, i * C : (i + 1) * C, :] + move * s


FIRST = range(MID // 2)
SECOND = range(COLS // 2)


def next_act(value, row, place):
    left = jnp.where(place[3] == 0, 0.0, 1.0)
    right = jnp.where(place[3] == NGY - 1, 0.0, 1.0)
    value = jnp.concatenate([value[0:1] * left, value[1 : MID - 1], value[MID - 1 :] * right], axis=0)
    if row == -1:
        value = value * jnp.where(place[2] == 0, 0.0, 1.0)
    if row == ROWS:
        value = value * jnp.where(place[2] == NGX - 1, 0.0, 1.0)
    return value.astype(BF16).reshape(MID * C, NT)


def inner_kernel(
    place, steps, act_own, base_own, cond, ya, yb, wide, wide_cond, wide_temporal, token,
    act, base, term, part1, part2, act2,
):
    del token
    factors = coefficients(steps[0], steps[1])
    lows, highs = halo_columns(place, ya, yb)
    for r in range(ROWS):
        low, high = lows(r), highs(r)
        x = jnp.concatenate([cells(low[0 : 2 * C]), cells(high[0 : 2 * C])], axis=0)
        fresh = jnp.concatenate([cells(low[2 * C : 3 * C]), cells(high[2 * C : 3 * C])], axis=0)
        done, value = prepare(x, fresh, factors)
        act[r, 0 : 2 * C, :] = done[0 : 2 * C]
        act[r, 2 * C : (WIDE - 2) * C, :] = act_own[r]
        act[r, (WIDE - 2) * C :, :] = done[2 * C :]
        base[r, 0:C, :] = value[0:C]
        base[r, C : (MID - 1) * C, :] = base_own[r]
        base[r, (MID - 1) * C :, :] = value[C:]
        field = wide_cond_row(cond[r], low, high).astype(F32)
        field = jnp.concatenate([field[CK * i : CK * (i + 1)] for i in range(MID)], axis=1).astype(BF16)
        term[r] = jnp.dot(wide_cond[0:FF, 0:CK], field, preferred_element_type=F32)
    for r in range(1, ROWS - 1):
        free = spatial_sum([(d + 1, pick(act, r + d)) for d in (-1, 0, 1)], FIRST, wide)
        add_sums(
            temporal_sum(free, free + cond_pairs(term[r], 0, MID // 2), wide_temporal), base, r, factors[1]
        )
    part1[0] = spatial_sum([(1, pick(act, 0)), (2, pick(act, 1))], FIRST, wide)
    part1[1] = spatial_sum([(0, pick(act, ROWS - 2)), (1, pick(act, ROWS - 1))], FIRST, wide)
    part1[2] = spatial_sum([(2, pick(act, 0))], FIRST, wide)
    part1[3] = spatial_sum([(0, pick(act, ROWS - 1))], FIRST, wide)
    for i in range(2):
        act2[i] = next_act(silu(normalize(base[1 + i].reshape(MID, C, NT))), 1 + i, place)
    one, two = pick(act2, 0), pick(act2, 1)
    part2[0] = spatial_sum([(2, one)], SECOND, wide)
    part2[1] = spatial_sum([(1, one), (2, two)], SECOND, wide)
    part2[2] = spatial_sum([(0, one), (1, two)], SECOND, wide)
    part2[3] = spatial_sum([(0, two)], SECOND, wide)


def inner(place, steps, act, base, cond, ya, yb, weights, token):
    return pl.pallas_call(
        inner_kernel,
        out_shape=(
            jax.ShapeDtypeStruct((ROWS, WIDE * C, NT), BF16),
            jax.ShapeDtypeStruct((ROWS, MID * C, NT), F32),
            jax.ShapeDtypeStruct((ROWS, FF, MID * NT), F32),
            jax.ShapeDtypeStruct((4, 2 * FF, MID // 2 * NT), F32),
            jax.ShapeDtypeStruct((4, 2 * FF, COLS // 2 * NT), F32),
            jax.ShapeDtypeStruct((2, MID * C, NT), BF16),
        ),
        in_specs=[smem(), smem()] + [vmem()] * 9,
        out_specs=(vmem(),) * 6,
        compiler_params=pltpu.CompilerParams(vmem_limit_bytes=VMEM_MOST),
        cost_estimate=pl.CostEstimate(flops=1 << 30, bytes_accessed=4 << 20, transcendentals=2 << 20),
        name="inner_rows",
    )(place, steps, act, base, cond, ya, yb, *weights, token)


def main_kernel(
    place, steps, noise, xb, xa, act, base_own, term, part1, part2, act2_own, wide, wide_cond, wide_temporal,
    out, outer, base, act2,
):
    factors = coefficients(steps[0], steps[1])
    even_x = place[0] == 0
    n = WIDE * C
    fields = []
    for top in (False, True):
        face = lambda lo, hi: jnp.where(even_x == top, xa[lo:hi, :], xb[lo:hi, :])
        near = 0 if top else 1
        for i in range(2):
            fresh = cells(face(2 * n, 2 * n + MID * C)) if i == near else None
            done, value = prepare(cells(face(i * n, (i + 1) * n)), fresh, factors)
            outer[2 * top + i] = done
            if i == near:
                base[2 + top] = value
        fields.append(face(2 * n + MID * C, XROWS))
    for i, r in enumerate((0, ROWS - 1)):
        base[i] = base_own[r]

    far = (
        [(0, pick(outer, 1))],
        [(2, pick(outer, 2))],
        [(0, pick(outer, 0)), (1, pick(outer, 1))],
        [(1, pick(outer, 2)), (2, pick(outer, 3))],
    )
    for slot in range(4):
        free = part1[slot] + spatial_sum(far[slot], FIRST, wide)
        if slot < 2:
            given = free + cond_pairs(term[(ROWS - 1) * slot], 0, MID // 2)
        else:
            field = jnp.concatenate([fields[slot - 2][2 * CK * p : 2 * CK * (p + 1)] for p in FIRST], axis=1)
            given = free + jnp.dot(wide_cond[...], field, preferred_element_type=F32)
        add_sums(temporal_sum(free, given, wide_temporal), base, slot, factors[1])

    keep2, move2, sigma2 = coefficients(steps[1], steps[2])
    slots = {0: 0, ROWS - 1: 1, -1: 2, ROWS: 3}
    for r in range(-1, ROWS + 1):
        x = (base[slots[r]] if r in slots else base_own[r]).reshape(MID, C, NT)
        normed = normalize(x)
        if r in slots:
            act2[slots[r]] = next_act(silu(normed), r, place)
        if 0 <= r < ROWS:
            out[r] = (
                keep2 * x[1 : MID - 1] + move2 * normed[1 : MID - 1] + sigma2 * noise[1, r].astype(F32)
            )

    near = (
        [(0, pick(act2, 2)), (1, pick(act2, 0))],
        [(0, pick(act2, 0))],
        [(2, pick(act2, 1))],
        [(1, pick(act2, 1)), (2, pick(act2, 3))],
    )
    for r in range(ROWS):
        free = part2[r] + spatial_sum(near[r], SECOND, wide)
        sums = temporal_sum(free, free + cond_pairs(term[r], 1, COLS // 2), wide_temporal)
        for i, s in enumerate(sums):
            out[r, i] = out[r, i] + move2 * s


def sample(place, steps, noise, xb, xa, parts, weights):
    return pl.pallas_call(
        main_kernel,
        out_shape=jax.ShapeDtypeStruct((ROWS, COLS, C, NT), F32),
        in_specs=[smem(), smem()] + [vmem()] * 12,
        out_specs=vmem(),
        scratch_shapes=[
            pltpu.VMEM((4, WIDE * C, NT), BF16),
            pltpu.VMEM((4, MID * C, NT), F32),
            pltpu.VMEM((4, MID * C, NT), BF16),
        ],
        compiler_params=pltpu.CompilerParams(vmem_limit_bytes=VMEM_MOST),
        cost_estimate=pl.CostEstimate(flops=2 << 30, bytes_accessed=5 << 20, transcendentals=5 << 20),
        name="sample_slab",
    )(place, steps, noise, xb, xa, *parts, *weights)


def on_device(latent, sample_noise, cond_field, timesteps, spatial_weight, cond_weight, temporal_weight):
    gx, gy = lax.axis_index("gx"), lax.axis_index("gy")
    place = jnp.stack([gx % 2, gy % 2, gx, gy]).astype(jnp.int32)
    cond = cond_field.reshape(ROWS, COLS * CK, NT)
    ya, yb, token = pack_y(place, latent, sample_noise, cond)
    ya = lax.ppermute(ya, AXES, swaps_y(0))
    yb = lax.ppermute(yb, AXES, swaps_y(1))
    act, base, packed = own(token, timesteps, latent, sample_noise)
    weights = widen(jnp.swapaxes(spatial_weight, 2, 3), cond_weight.T, temporal_weight)
    xb, xa, token = pack_x(place, packed, sample_noise, cond, ya, yb)
    xb = lax.ppermute(xb, AXES, swaps_x(1))
    xa = lax.ppermute(xa, AXES, swaps_x(0))
    parts = inner(place, timesteps, act, base, cond, ya, yb, weights, token)
    return sample(place, timesteps, sample_noise, xb, xa, parts, weights)


def solution(mesh):
    in_specs = (
        P("gx", "gy", None, None),
        P(None, "gx", "gy", None, None),
        P("gx", "gy", None, None),
        P(),
        P(),
        P(),
        P(),
    )
    return jax.shard_map(
        on_device, mesh=mesh, in_specs=in_specs, out_specs=P("gx", "gy", None, None), check_vma=False
    )
```

```python
import jax
import jax.numpy as jnp
from jax import lax
from jax.experimental import pallas as pl
from jax.experimental.pallas import tpu as pltpu
from jax.sharding import PartitionSpec as P

F32 = jnp.float32
BF16 = jnp.bfloat16
VMEM_ALL = 52 << 20
VMEM_MOST = 34 << 20
AXES = ("cfg", "gx", "gy")
NCFG, NGX, NGY = 2, 16, 8
ROWS, COLS, C, FF, CK, NT = 4, 16, 32, 128, 8, 128
YROWS = 2 * C + C + 2 * CK
WIDE, MID = COLS + 4, COLS + 2
XROWS = 2 * WIDE * C + MID * C + MID * CK


def linear(cfg, gx, gy):
    return (cfg * NGX + gx) * NGY + gy


def swaps_x(parity):
    pairs = []
    for cfg in range(NCFG):
        for gy in range(NGY):
            for gx in range(parity, NGX - 1, 2):
                other = 1 - cfg if gx == NGX // 2 - 1 else cfg
                a, b = linear(cfg, gx, gy), linear(other, gx + 1, gy)
                pairs += [(a, b), (b, a)]
    return pairs


def swaps_y(parity):
    pairs = []
    for cfg in range(NCFG):
        for gx in range(NGX):
            for gy in range(parity, NGY - 1, 2):
                a, b = linear(cfg, gx, gy), linear(cfg, gx, gy + 1)
                pairs += [(a, b), (b, a)]
    return pairs


def vmem():
    return pl.BlockSpec(memory_space=pltpu.VMEM)


def smem():
    return pl.BlockSpec(memory_space=pltpu.SMEM)


def join16(*parts):
    return jnp.concatenate([p.astype(F32) for p in parts], axis=0).astype(BF16)


def any_space():
    return pl.BlockSpec(memory_space=pl.ANY)


def cells(v):
    return v.astype(F32).reshape(-1, C, NT)


def pack_y_kernel(place, lat, noise, cond, ya, yb, token, xs, ns, cs, sems):
    token[...] = jnp.zeros(token.shape, F32)
    copies = []
    for side, (lo, inner, field) in enumerate(((0, 0, 0), (COLS - 2, COLS - 1, (COLS - 2) * CK))):
        copies.append(pltpu.make_async_copy(lat.at[:, lo : lo + 2], xs.at[side], sems.at[3 * side]))
        copies.append(pltpu.make_async_copy(noise.at[0, :, inner], ns.at[side], sems.at[3 * side + 1]))
        copies.append(
            pltpu.make_async_copy(cond.at[:, field : field + 2 * CK, :], cs.at[side], sems.at[3 * side + 2])
        )
    for copy in copies:
        copy.start()
    for copy in copies:
        copy.wait()

    def pack_y(out, side):
        for r in range(ROWS):
            out[r, 0 : 2 * C, :] = xs[side, r].reshape(2 * C, NT).astype(BF16)
            out[r, 2 * C : 3 * C, :] = ns[side, r]
            both = cs[side, r].astype(F32)
            cell = both[CK:] if side else both[0:CK]
            out[r, 3 * C :, :] = join16(cell, cell)

    for parity in range(2):

        @pl.when(place[1] == parity)
        def _():
            pack_y(ya, 1 - parity)
            pack_y(yb, parity)


def pack_y(place, lat, noise, cond):
    y = jax.ShapeDtypeStruct((ROWS, YROWS, NT), BF16)
    return pl.pallas_call(
        pack_y_kernel,
        out_shape=(y, y, jax.ShapeDtypeStruct((8, NT), F32)),
        in_specs=[smem(), any_space(), any_space(), any_space()],
        out_specs=(vmem(),) * 3,
        scratch_shapes=[
            pltpu.VMEM((2, ROWS, 2, C, NT), F32),
            pltpu.VMEM((2, ROWS, C, NT), BF16),
            pltpu.VMEM((2, ROWS, 2 * CK, NT), BF16),
            pltpu.SemaphoreType.DMA((6,)),
        ],
        compiler_params=pltpu.CompilerParams(vmem_limit_bytes=VMEM_ALL),
        cost_estimate=pl.CostEstimate(flops=1 << 16, bytes_accessed=1 << 19, transcendentals=0),
        name="pack_columns",
    )(place, lat, noise, cond)


def halo_columns(place, ya, yb):
    even = place[1] == 0
    return (
        lambda r: jnp.where(even, yb[r], ya[r]),
        lambda r: jnp.where(even, ya[r], yb[r]),
    )


def own_kernel(token, steps, lat, noise, act, base, packed):
    del token
    factors = coefficients(steps[0], steps[1])
    for r in range(ROWS):
        x = lat[r]
        packed[r] = x.astype(BF16).reshape(COLS * C, NT)
        act[r], base[r] = prepare(x, noise[0, r], factors)


def own(token, steps, lat, noise):
    n = COLS * C
    return pl.pallas_call(
        own_kernel,
        out_shape=(
            jax.ShapeDtypeStruct((ROWS, n, NT), BF16),
            jax.ShapeDtypeStruct((ROWS, n, NT), F32),
            jax.ShapeDtypeStruct((ROWS, n, NT), BF16),
        ),
        in_specs=[vmem(), smem(), vmem(), vmem()],
        out_specs=(vmem(),) * 3,
        compiler_params=pltpu.CompilerParams(vmem_limit_bytes=24 << 20),
        cost_estimate=pl.CostEstimate(flops=1 << 24, bytes_accessed=4 << 20, transcendentals=1 << 18),
        name="own_cells",
    )(token, steps, lat, noise)


def wide_cond_row(cond_row, low, high):
    return join16(low.astype(F32)[3 * C : 3 * C + CK], cond_row, high.astype(F32)[3 * C : 3 * C + CK])


def pack_x_kernel(place, packed, noise, cond, ya, yb, xb, xa, token):
    lows, highs = halo_columns(place, ya, yb)

    def pack_x(out, top):
        lo, inner = (ROWS - 2, ROWS - 1) if top else (0, 0)
        n = WIDE * C
        for i in range(2):
            low, high = lows(lo + i), highs(lo + i)
            out[i * n : i * n + 2 * C, :] = low[0 : 2 * C]
            out[i * n + 2 * C : (i + 1) * n - 2 * C, :] = packed[lo + i]
            out[(i + 1) * n - 2 * C : (i + 1) * n, :] = high[0 : 2 * C]
            if lo + i == inner:
                at, end = 2 * n, 2 * n + MID * C
                out[at : at + C, :] = low[2 * C : 3 * C]
                out[at + C : end - C, :] = noise[0, inner].reshape(COLS * C, NT)
                out[end - C : end, :] = high[2 * C : 3 * C]
                out[end:, :] = wide_cond_row(cond[inner], low, high)

    for parity in range(2):

        @pl.when(place[0] == parity)
        def _():
            pack_x(xa, parity == 0)
            pack_x(xb, parity == 1)

    token[...] = jnp.zeros(token.shape, F32)


def pack_x(place, packed, noise, cond, ya, yb):
    x = jax.ShapeDtypeStruct((XROWS, NT), BF16)
    return pl.pallas_call(
        pack_x_kernel,
        out_shape=(x, x, jax.ShapeDtypeStruct((8, NT), F32)),
        in_specs=[smem()] + [vmem()] * 5,
        out_specs=(vmem(),) * 3,
        compiler_params=pltpu.CompilerParams(vmem_limit_bytes=24 << 20),
        cost_estimate=pl.CostEstimate(flops=1 << 18, bytes_accessed=3 << 20, transcendentals=0),
        name="pack_rows",
    )(place, packed, noise, cond, ya, yb)


def weights_kernel(spatial, cond, temporal, wide, wide_cond, wide_temporal):
    blank = jnp.zeros((C, FF), F32)
    for dx in range(3):
        taps = [0.5 * spatial[dx, dy].astype(F32) for dy in range(3)]
        at = slice(dx * 4 * C, (dx + 1) * 4 * C)
        wide[0:FF, at] = jnp.concatenate(taps + [blank], axis=0).T.astype(BF16)
        wide[FF:, at] = jnp.concatenate([blank] + taps, axis=0).T.astype(BF16)
    small = 0.5 * cond[...].astype(F32)
    none = jnp.zeros((FF - CK, FF), F32)
    pair = jnp.concatenate([small, none], axis=0).T[:, 0:CK]
    gap = jnp.zeros((FF, CK), F32)
    wide_cond[0:FF, :] = jnp.concatenate([pair, gap], axis=1).astype(BF16)
    wide_cond[FF:, :] = jnp.concatenate([gap, pair], axis=1).astype(BF16)
    wide_temporal[...] = jnp.zeros(wide_temporal.shape, BF16)
    wide_temporal[0 : 3 * C, 0:FF] = (2.0 * temporal[...].astype(F32)).astype(BF16).reshape(3 * C, FF)
    wide_temporal[3 * C :, FF:] = (2.0 * temporal[...].astype(F32)).astype(BF16).reshape(3 * C, FF)


def widen(spatial, cond, temporal):
    return pl.pallas_call(
        weights_kernel,
        out_shape=(
            jax.ShapeDtypeStruct((2 * FF, 12 * C), BF16),
            jax.ShapeDtypeStruct((2 * FF, 2 * CK), BF16),
            jax.ShapeDtypeStruct((6 * C, 2 * FF), BF16),
        ),
        in_specs=[vmem()] * 3,
        out_specs=(vmem(),) * 3,
        compiler_params=pltpu.CompilerParams(vmem_limit_bytes=16 << 20),
        cost_estimate=pl.CostEstimate(flops=1 << 18, bytes_accessed=1 << 20, transcendentals=0),
        name="widen_weights",
    )(spatial, cond, temporal)


def log_alpha(when):
    shape = (8, 128)
    position = lax.broadcasted_iota(jnp.int32, shape, 0) * 128 + lax.broadcasted_iota(jnp.int32, shape, 1)
    beta = 0.0001 + (0.02 - 0.0001) * position.astype(F32) / 999.0
    logs = jnp.log(1.0 - jnp.minimum(beta, 0.5))
    return jnp.sum(jnp.where(position <= when, logs, 0.0))


def coefficients(now, later):
    a = jnp.exp(jnp.full((1, NT), log_alpha(now), F32))
    p = jnp.exp(jnp.full((1, NT), log_alpha(later), F32))
    sigma = 0.5 * jnp.sqrt((1.0 - p) / (1.0 - a)) * jnp.sqrt(1.0 - a / p)
    keep = jnp.sqrt(p) / jnp.sqrt(a)
    move = jnp.sqrt(1.0 - p - sigma * sigma) - keep * jnp.sqrt(1.0 - a)
    return keep, move, sigma


def silu(v):
    half = 0.5 * v
    return half + half * jnp.tanh(half)


def normalize(x):
    mean = jnp.sum(jnp.sum(x * x, axis=1, keepdims=True), axis=2, keepdims=True) * (1.0 / (C * NT))
    return x * lax.rsqrt(mean + 1e-05)


def spatial_sum(terms, pairs, wide):
    windows = [
        jnp.concatenate([row(2 * C * p, 2 * C * p + 4 * C) for _, row in terms], axis=0) for p in pairs
    ]
    taps = wide[:, 4 * C * terms[0][0] : 4 * C * (terms[-1][0] + 1)]
    return jnp.dot(taps, jnp.concatenate(windows, axis=1), preferred_element_type=F32)


def cond_pairs(term, first, pairs):
    cell = lambda i: term[:, NT * (first + i) : NT * (first + i + 1)]
    return jnp.concatenate(
        [jnp.concatenate([cell(2 * p), cell(2 * p + 1)], axis=0) for p in range(pairs)], axis=1
    )


def temporal_sum(free, given, wide_temporal):
    pairs = range(free.shape[1] // NT)
    given = given.astype(BF16)
    free = free.astype(BF16)
    hidden = (given + given * jnp.tanh(given)) * BF16(1.5) - (free + free * jnp.tanh(free))
    taps = jnp.dot(wide_temporal[...], hidden, preferred_element_type=F32)
    time = lax.broadcasted_iota(jnp.int32, (C, NT), 1)
    sums = []
    for q in pairs:
        for o in range(2):
            t = taps[3 * C * o : 3 * C * (o + 1), NT * q : NT * (q + 1)]
            before = jnp.where(time == 0, 0.0, pltpu.roll(t[0:C], 1, 1))
            after = jnp.where(time == NT - 1, 0.0, pltpu.roll(t[2 * C :], NT - 1, 1))
            sums.append(before + t[C : 2 * C] + after)
    return sums


def prepare(x, fresh, factors):
    normed = normalize(x)
    act = silu(normed).astype(BF16).reshape(-1, NT)
    if fresh is None:
        return act, None
    keep, move, sigma = factors
    skip = (x.shape[0] - fresh.shape[0]) // 2
    part = slice(skip, skip + fresh.shape[0])
    value = keep * x[part] + move * normed[part] + sigma * fresh.astype(F32)
    return act, value.reshape(-1, NT)


def pick(ref, *lead):
    return lambda lo, hi: ref[(*lead, slice(lo, hi), slice(None))]


def add_sums(sums, base, e, move):
    for i, s in enumerate(sums):
        base[e, i * C : (i + 1) * C, :] = base[e, i * C : (i + 1) * C, :] + move * s


FIRST = range(MID // 2)
SECOND = range(COLS // 2)


def next_base(x, normed, fresh, factors):
    keep, move, sigma = factors
    return keep * x[1 : MID - 1] + move * normed[1 : MID - 1] + sigma * fresh.astype(F32)


def next_act(value, row, place):
    left = jnp.where(place[3] == 0, 0.0, 1.0)
    right = jnp.where(place[3] == NGY - 1, 0.0, 1.0)
    value = jnp.concatenate([value[0:1] * left, value[1 : MID - 1], value[MID - 1 :] * right], axis=0)
    if row == -1:
        value = value * jnp.where(place[2] == 0, 0.0, 1.0)
    if row == ROWS:
        value = value * jnp.where(place[2] == NGX - 1, 0.0, 1.0)
    return value.astype(BF16).reshape(MID * C, NT)


def inner_kernel(
    place, steps, act_own, base_own, noise, cond, ya, yb, wide, wide_cond, wide_temporal, token,
    act, base, term, part1, part2, act2, base2,
):
    del token
    factors = coefficients(steps[0], steps[1])
    lows, highs = halo_columns(place, ya, yb)
    for r in range(ROWS):
        low, high = lows(r), highs(r)
        x = jnp.concatenate([cells(low[0 : 2 * C]), cells(high[0 : 2 * C])], axis=0)
        fresh = jnp.concatenate([cells(low[2 * C : 3 * C]), cells(high[2 * C : 3 * C])], axis=0)
        done, value = prepare(x, fresh, factors)
        act[r, 0 : 2 * C, :] = done[0 : 2 * C]
        act[r, 2 * C : (WIDE - 2) * C, :] = act_own[r]
        act[r, (WIDE - 2) * C :, :] = done[2 * C :]
        base[r, 0:C, :] = value[0:C]
        base[r, C : (MID - 1) * C, :] = base_own[r]
        base[r, (MID - 1) * C :, :] = value[C:]
        field = wide_cond_row(cond[r], low, high).astype(F32)
        field = jnp.concatenate([field[CK * i : CK * (i + 1)] for i in range(MID)], axis=1).astype(BF16)
        term[r] = jnp.dot(wide_cond[0:FF, 0:CK], field, preferred_element_type=F32)
    for r in range(1, ROWS - 1):
        free = spatial_sum([(d + 1, pick(act, r + d)) for d in (-1, 0, 1)], FIRST, wide)
        add_sums(
            temporal_sum(free, free + cond_pairs(term[r], 0, MID // 2), wide_temporal), base, r, factors[1]
        )
    part1[0] = spatial_sum([(1, pick(act, 0)), (2, pick(act, 1))], FIRST, wide)
    part1[1] = spatial_sum([(0, pick(act, ROWS - 2)), (1, pick(act, ROWS - 1))], FIRST, wide)
    part1[2] = spatial_sum([(2, pick(act, 0))], FIRST, wide)
    part1[3] = spatial_sum([(0, pick(act, ROWS - 1))], FIRST, wide)
    later = coefficients(steps[1], steps[2])
    for i in range(2):
        x = base[1 + i].reshape(MID, C, NT)
        normed = normalize(x)
        act2[i] = next_act(silu(normed), 1 + i, place)
        base2[i] = next_base(x, normed, noise[1, 1 + i], later)
    one, two = pick(act2, 0), pick(act2, 1)
    part2[0] = spatial_sum([(2, one)], SECOND, wide)
    part2[1] = spatial_sum([(1, one), (2, two)], SECOND, wide)
    part2[2] = spatial_sum([(0, one), (1, two)], SECOND, wide)
    part2[3] = spatial_sum([(0, two)], SECOND, wide)


def inner(place, steps, act, base, noise, cond, ya, yb, weights, token):
    return pl.pallas_call(
        inner_kernel,
        out_shape=(
            jax.ShapeDtypeStruct((ROWS, WIDE * C, NT), BF16),
            jax.ShapeDtypeStruct((ROWS, MID * C, NT), F32),
            jax.ShapeDtypeStruct((ROWS, FF, MID * NT), F32),
            jax.ShapeDtypeStruct((4, 2 * FF, MID // 2 * NT), F32),
            jax.ShapeDtypeStruct((4, 2 * FF, COLS // 2 * NT), F32),
            jax.ShapeDtypeStruct((2, MID * C, NT), BF16),
            jax.ShapeDtypeStruct((2, COLS, C, NT), F32),
        ),
        in_specs=[smem(), smem()] + [vmem()] * 10,
        out_specs=(vmem(),) * 7,
        compiler_params=pltpu.CompilerParams(vmem_limit_bytes=VMEM_MOST),
        cost_estimate=pl.CostEstimate(flops=1 << 30, bytes_accessed=4 << 20, transcendentals=2 << 20),
        name="inner_rows",
    )(place, steps, act, base, noise, cond, ya, yb, *weights, token)


def main_kernel(
    place, steps, noise, xb, xa, act, base_own, term, part1, part2, act2_own, base2_own, wide, wide_cond, wide_temporal,
    out, outer, base, act2,
):
    factors = coefficients(steps[0], steps[1])
    even_x = place[0] == 0
    n = WIDE * C
    fields = []
    for top in (False, True):
        face = lambda lo, hi: jnp.where(even_x == top, xa[lo:hi, :], xb[lo:hi, :])
        near = 0 if top else 1
        for i in range(2):
            fresh = cells(face(2 * n, 2 * n + MID * C)) if i == near else None
            done, value = prepare(cells(face(i * n, (i + 1) * n)), fresh, factors)
            outer[2 * top + i] = done
            if i == near:
                base[2 + top] = value
        fields.append(face(2 * n + MID * C, XROWS))
    for i, r in enumerate((0, ROWS - 1)):
        base[i] = base_own[r]

    far = (
        [(0, pick(outer, 1))],
        [(2, pick(outer, 2))],
        [(0, pick(outer, 0)), (1, pick(outer, 1))],
        [(1, pick(outer, 2)), (2, pick(outer, 3))],
    )
    for slot in range(4):
        free = part1[slot] + spatial_sum(far[slot], FIRST, wide)
        if slot < 2:
            given = free + cond_pairs(term[(ROWS - 1) * slot], 0, MID // 2)
        else:
            field = jnp.concatenate([fields[slot - 2][2 * CK * p : 2 * CK * (p + 1)] for p in FIRST], axis=1)
            given = free + jnp.dot(wide_cond[...], field, preferred_element_type=F32)
        add_sums(temporal_sum(free, given, wide_temporal), base, slot, factors[1])

    later = coefficients(steps[1], steps[2])
    for r, slot in ((0, 0), (ROWS - 1, 1), (-1, 2), (ROWS, 3)):
        x = base[slot].reshape(MID, C, NT)
        normed = normalize(x)
        act2[slot] = next_act(silu(normed), r, place)
        if slot < 2:
            out[r] = next_base(x, normed, noise[1, r], later)

    near = (
        [(0, pick(act2, 2)), (1, pick(act2, 0))],
        [(0, pick(act2, 0))],
        [(2, pick(act2, 1))],
        [(1, pick(act2, 1)), (2, pick(act2, 3))],
    )
    for r in range(ROWS):
        free = part2[r] + spatial_sum(near[r], SECOND, wide)
        sums = temporal_sum(free, free + cond_pairs(term[r], 1, COLS // 2), wide_temporal)
        for i, s in enumerate(sums):
            own_part = base2_own[r - 1, i] if 0 < r < ROWS - 1 else out[r, i]
            out[r, i] = own_part + later[1] * s


def sample(place, steps, noise, xb, xa, parts, weights):
    return pl.pallas_call(
        main_kernel,
        out_shape=jax.ShapeDtypeStruct((ROWS, COLS, C, NT), F32),
        in_specs=[smem(), smem()] + [vmem()] * 13,
        out_specs=vmem(),
        scratch_shapes=[
            pltpu.VMEM((4, WIDE * C, NT), BF16),
            pltpu.VMEM((4, MID * C, NT), F32),
            pltpu.VMEM((4, MID * C, NT), BF16),
        ],
        compiler_params=pltpu.CompilerParams(vmem_limit_bytes=VMEM_MOST),
        cost_estimate=pl.CostEstimate(flops=2 << 30, bytes_accessed=5 << 20, transcendentals=5 << 20),
        name="sample_slab",
    )(place, steps, noise, xb, xa, *parts, *weights)


def on_device(latent, sample_noise, cond_field, timesteps, spatial_weight, cond_weight, temporal_weight):
    gx, gy = lax.axis_index("gx"), lax.axis_index("gy")
    place = jnp.stack([gx % 2, gy % 2, gx, gy]).astype(jnp.int32)
    cond = cond_field.reshape(ROWS, COLS * CK, NT)
    ya, yb, token = pack_y(place, latent, sample_noise, cond)
    ya = lax.ppermute(ya, AXES, swaps_y(0))
    yb = lax.ppermute(yb, AXES, swaps_y(1))
    act, base, packed = own(token, timesteps, latent, sample_noise)
    weights = widen(jnp.swapaxes(spatial_weight, 2, 3), cond_weight.T, temporal_weight)
    xb, xa, token = pack_x(place, packed, sample_noise, cond, ya, yb)
    xb = lax.ppermute(xb, AXES, swaps_x(1))
    xa = lax.ppermute(xa, AXES, swaps_x(0))
    parts = inner(place, timesteps, act, base, sample_noise, cond, ya, yb, weights, token)
    return sample(place, timesteps, sample_noise, xb, xa, parts, weights)


def solution(mesh):
    in_specs = (
        P("gx", "gy", None, None),
        P(None, "gx", "gy", None, None),
        P("gx", "gy", None, None),
        P(),
        P(),
        P(),
        P(),
    )
    return jax.shard_map(
        on_device, mesh=mesh, in_specs=in_specs, out_specs=P("gx", "gy", None, None), check_vma=False
    )
```
